32 devices in a mesh: expert: 16 (over z, y, core), dp: 2 (over x).
Axes of the slice: x: 2, y: 2, z: 4, core: 2. Of those that a mesh axis runs over, the one named last changes fastest.
Arguments:
- tokens: bfloat16 [1024, 2048], P(('expert', 'dp')), may hold values from -6 to 6
- expert_ids: int32 [1024, 8], P(('expert', 'dp')), may hold values from 0 to 15, all different within a row; in each aligned block of 32 rows (0 to 31, 32 to 63, ...) at most 32 rows name the same one
- gate_weights: bfloat16 [1024, 8], P(('expert', 'dp')), may hold values from 0.049804688 to 0.25
- cotangent: bfloat16 [1024, 2048], P(('expert', 'dp')), may hold values from -12 to 12
- w_gate: bfloat16 [16, 768, 2048], P('expert'), may hold values from -0.125 to 0.125
- w_up: bfloat16 [16, 768, 2048], P('expert'), may hold values from -0.125 to 0.125
- w_down: bfloat16 [16, 2048, 768], P('expert'), may hold values from -0.21875 to 0.21875
Outputs:
- token_grad: bfloat16 [1024, 2048], P(('expert', 'dp'))
- gate_grad: bfloat16 [1024, 8], P(('expert', 'dp'))
- grad_gate: bfloat16 [16, 768, 2048], P('expert', 'dp')
- grad_up: bfloat16 [16, 768, 2048], P('expert', 'dp')
- grad_down_t: bfloat16 [16, 768, 2048], P('expert', 'dp')
The draws below stay inside these ranges and needn't reach their ends.
Inputs may be any that keep to these rules, and one draw needn't show every extreme that they name: `expert_ids`: each token names 8 different experts. Among the tokens of one device (aligned blocks of 32 rows), no expert is named by more than 32 of them, a bound that some block reaches.
All inputs are finite; a program needn't handle non-finite values.
Results may differ from the reference program's by a relative error of at most 0.017.
Values may be sent and summed in bfloat16 or wider, within the bound.
No kernel may reach another device: no remote copies, remote signals or barrier semaphores. Data moves between devices by JAX's collectives and lax.ppermute only.
A program may use at most 128 MiB of HBM per device.

```python
import math
import jax
import jax.numpy as jnp
import numpy as np
from jax import lax

D = 2048
H = 768
TOP = 8
TOK_DEV = 32
EXPERTS = 16
CAP = 32
TOKENS = 1024
N_EXPERT = 16
N_DP = 2


def steps_of(key, dims, shards, smallest, largest):
    def one(dim, shards_of):
        heights = jax.random.uniform(jax.random.fold_in(jax.random.fold_in(key, 6), dim), (shards_of,), jnp.float32, smallest / len(shards), largest / len(shards))
        return jnp.repeat(jnp.exp(heights), dims[dim] // shards_of).reshape((-1,) + (1,) * (len(dims) - dim - 1))

    level = one(*shards[0])
    for cut in shards[1:]:
        level = level * one(*cut)
    return level


def routed_block(rng, own, number, rows, count, top, bound, skew):
    sequence = jax.random.permutation(rng, count)
    packed, ordinary = shares(count, rows * top, bound, skew, True), shares(count, rows * top, bound, skew, False)
    places = jnp.arange(count)

    def named(sizes, rotation):
        used = int((sizes > 0).sum())
        fixed = max(1, used // 4)
        shifted = fixed + (places - fixed + rotation * (used - fixed)) % max(1, count - fixed)
        return jnp.zeros((count,), jnp.int32).at[sequence[jnp.where(places < fixed, places, shifted)]].set(jnp.asarray(sizes, jnp.int32))

    sizes = jnp.where(number % 4 == 0, named(packed, number // 4), named(ordinary, number - number // 4 - 1))
    mixed = jax.random.permutation(jax.random.fold_in(own, 3), count)
    source_of, taker = mixed[0:count // 2 * 2:2], mixed[1:count // 2 * 2:2]
    margin = jnp.minimum(sizes[source_of] - 1, bound - sizes[taker]) // 2
    margin = jnp.where((source_of == sequence[0]) | (taker == sequence[0]) | (sizes[taker] == 0), 0, jnp.maximum(margin, 0))
    shifted = jax.random.randint(jax.random.fold_in(own, 4), (count // 2,), 0, 1 << 20) % (margin + 1)
    sizes = sizes.at[source_of].add(-shifted).at[taker].add(shifted)
    items = jnp.searchsorted(jnp.cumsum(sizes), jnp.arange(rows * top), side="right").astype(jnp.int32)
    table = items.reshape(top, rows).T
    table = table[jax.random.permutation(jax.random.fold_in(own, 1), rows)]
    rotation = jax.random.randint(jax.random.fold_in(own, 2), (rows, 1), 0, top)
    return jnp.take_along_axis(table, (jnp.arange(top)[None, :] + rotation) % top, axis=1)


def shares(number_of, total, most, lean, full):
    weights = [(1 << 20) // math.isqrt(rank ** lean) + 1 for rank in range(1, number_of + 1)]
    largest = most if full else min(most, max(-(-total // number_of), total * weights[0] // sum(weights)))
    least = 1 if total - largest >= number_of - 1 else 0
    counts, surplus = [largest] + [least] * (number_of - 1), total - largest - least * (number_of - 1)
    while surplus > 0:
        free = [i for i in range(1, number_of) if counts[i] < largest] or [i for i in range(1, number_of) if counts[i] < most]
        mass, budget = sum([weights[i] for i in free]), surplus
        for i in free:
            more = min(most - counts[i], max(1, budget * weights[i] // mass), surplus)
            counts[i] = counts[i] + more
            surplus = surplus - more
    return np.array(counts)


def centred(rng, shape, width, limit, pieces=(), kind=jnp.bfloat16):
    entries = jax.random.normal(rng, shape, jnp.float32) * width
    if len(pieces) > 0:
        entries = steps_of(rng, shape, pieces, -0.22, 0.18) * entries
    return jnp.clip(entries, min=-limit, max=limit).astype(kind)


def setup_inputs(seed: int = 0) -> dict:
    seeds = jax.random.split(jax.random.key(seed), 8)
    tokens = centred(seeds[0], (TOKENS, D), 1.0, 6.0, ((0, 32),))
    expert_ids_keys = jax.random.split(jax.random.fold_in(seeds[1], 1), TOKENS // TOK_DEV)
    expert_ids_turns = jax.random.permutation(jax.random.fold_in(seeds[1], 3), TOKENS // TOK_DEV)
    expert_ids = jax.vmap(lambda own, number: routed_block(jax.random.fold_in(seeds[1], 2), own, number, TOK_DEV, EXPERTS, TOP, CAP, 2))(expert_ids_keys, expert_ids_turns).reshape((TOKENS, TOP))
    gate_weights = jnp.clip(0.049804688 + 0.20019531 * jax.random.uniform(seeds[2], (TOKENS, TOP), jnp.float32) ** steps_of(seeds[2], (TOKENS, TOP), ((0, 32),), -0.2, 0.2), 0.049804688, 0.25).astype(jnp.bfloat16)
    cotangent = centred(seeds[3], (TOKENS, D), 2.0, 12.0, ((0, 32),))
    w_gate = centred(seeds[4], (EXPERTS, H, D), D ** -0.5, 0.125, ((0, 16),))
    w_up = centred(seeds[5], (EXPERTS, H, D), D ** -0.5, 0.125, ((0, 16),))
    w_down = centred(seeds[6], (EXPERTS, D, H), H ** -0.5, 0.21875, ((0, 16),))
    return dict(tokens=tokens, expert_ids=expert_ids, gate_weights=gate_weights, cotangent=cotangent, w_gate=w_gate, w_up=w_up, w_down=w_down)


def contract_last(left, right):
    return lax.dot_general(left, right, (((1,), (1,)), ((), ())), preferred_element_type=jnp.float32)


def contract_first(left, right):
    return lax.dot_general(left, right, (((0,), (0,)), ((), ())), preferred_element_type=jnp.float32)


def rounded(value):
    return lax.optimization_barrier(value.astype(jnp.bfloat16)).astype(jnp.float32)


def expert_forward(expert_rows, gate_mat, up_mat, down_mat):
    pre_gate = contract_last(expert_rows, gate_mat)
    pre_up = contract_last(expert_rows, up_mat)
    gate_sigmoid = jax.nn.sigmoid(pre_gate)
    hidden = (pre_gate * gate_sigmoid * pre_up).astype(jnp.bfloat16)
    outputs = contract_last(hidden, down_mat).astype(jnp.bfloat16)
    return pre_gate, pre_up, gate_sigmoid, hidden, outputs


def reference(tokens, expert_ids, gate_weights, cotangent, w_gate, w_up, w_down):
    blocks = TOKENS // TOK_DEV
    slot_count = TOK_DEV * TOP
    buffer_rows = N_EXPERT * CAP
    block_ids = expert_ids.reshape(blocks, slot_count)
    onehot = (block_ids[:, :, None] == jnp.arange(EXPERTS, dtype=jnp.int32)[None, None, :]).astype(jnp.int32)
    slot_rank = jnp.sum((jnp.cumsum(onehot, axis=1) - 1) * onehot, axis=2).astype(jnp.int32)
    block_index = jnp.arange(blocks, dtype=jnp.int32)[:, None] * jnp.ones((1, slot_count), jnp.int32)
    group_index = block_index % N_DP
    source_index = block_index // N_DP
    slot_index = block_index * slot_count + jnp.arange(slot_count, dtype=jnp.int32)[None, :]
    table = jnp.full((N_DP, EXPERTS, N_EXPERT, CAP), -1, jnp.int32)
    table = table.at[group_index, block_ids, source_index, slot_rank].set(slot_index)
    table_by_expert = jnp.transpose(table, (1, 0, 2, 3))
    flat_gates = gate_weights.reshape(-1)

    def per_expert(carry, inputs):
        token_acc, score_acc = carry
        gate_mat, up_mat, down_mat, entry = inputs
        sums = [jnp.zeros((H, D), jnp.float32) for _ in range(3)]
        for group_id in range(N_DP):
            index = entry[group_id].reshape(buffer_rows)
            valid = index >= 0
            safe = jnp.maximum(index, 0).astype(jnp.int32)
            token_id = (safe // TOP).astype(jnp.int32)
            expert_rows = jnp.where(valid[:, None], tokens[token_id], jnp.zeros((), jnp.bfloat16))
            cot_rows = cotangent[token_id]
            gate_rows = jnp.where(valid, flat_gates[safe].astype(jnp.float32), jnp.zeros((), jnp.float32))
            pre_gate, pre_up, gate_sigmoid, hidden, outputs = expert_forward(expert_rows, gate_mat, up_mat, down_mat)
            score = jnp.sum(outputs.astype(jnp.float32) * cot_rows.astype(jnp.float32), axis=1)
            scaled = (gate_rows[:, None] * cot_rows.astype(jnp.float32)).astype(jnp.bfloat16)
            d_hidden = jnp.dot(scaled, down_mat, preferred_element_type=jnp.float32)
            d_pre_gate = (d_hidden * pre_up * gate_sigmoid * (1.0 + pre_gate * (1.0 - gate_sigmoid))).astype(jnp.bfloat16)
            d_pre_up = (d_hidden * pre_gate * gate_sigmoid).astype(jnp.bfloat16)
            slot_grad = (jnp.dot(d_pre_gate, gate_mat, preferred_element_type=jnp.float32)
                         + jnp.dot(d_pre_up, up_mat, preferred_element_type=jnp.float32)).astype(jnp.bfloat16)
            token_acc = token_acc.at[token_id].add(jnp.where(valid[:, None], slot_grad.astype(jnp.float32), jnp.zeros((), jnp.float32)))
            score_acc = score_acc.at[safe].add(jnp.where(valid, score, jnp.zeros((), jnp.float32)))
            sums[0] = sums[0] + rounded(contract_first(d_pre_gate, expert_rows))
            sums[1] = sums[1] + rounded(contract_first(d_pre_up, expert_rows))
            sums[2] = sums[2] + rounded(contract_first(hidden, scaled))
        return (token_acc, score_acc), (sums[0].astype(jnp.bfloat16), sums[1].astype(jnp.bfloat16), sums[2].astype(jnp.bfloat16))

    start = (jnp.zeros((TOKENS, D), jnp.float32), jnp.zeros((TOKENS * TOP,), jnp.float32))
    (token_acc, score_acc), (grad_gate, grad_up, grad_down_t) = lax.scan(
        per_expert, start, (w_gate, w_up, w_down, table_by_expert))
    token_grad = token_acc.astype(jnp.bfloat16)
    gate_grad = score_acc.reshape(TOKENS, TOP).astype(jnp.bfloat16)
    return (token_grad, gate_grad, grad_gate, grad_up, grad_down_t)
```

```python
import jax
import jax.numpy as jnp
from jax import lax
from jax.sharding import PartitionSpec as P

BOTH = ("expert", "dp")


def contract_last(left, right):
    return lax.dot_general(
        left, right, (((1,), (1,)), ((), ())), preferred_element_type=jnp.float32
    )


def contract_first(left, right):
    return lax.dot_general(
        left, right, (((0,), (0,)), ((), ())), preferred_element_type=jnp.float32
    )


def rounded(value):
    return lax.optimization_barrier(value.astype(jnp.bfloat16)).astype(jnp.float32)


def expert_forward(expert_rows, gate_mat, up_mat, down_mat):
    pre_gate = contract_last(expert_rows, gate_mat)
    pre_up = contract_last(expert_rows, up_mat)
    gate_sigmoid = jax.nn.sigmoid(pre_gate)
    hidden = (pre_gate * gate_sigmoid * pre_up).astype(jnp.bfloat16)
    outputs = contract_last(hidden, down_mat).astype(jnp.bfloat16)
    return (pre_gate, pre_up, gate_sigmoid, hidden, outputs)


def routed_body(tokens, expert_ids, gate_weights, cotangent, w_gate, w_up, w_down):
    tok_rows, top_count = expert_ids.shape
    model_width = tokens.shape[1]
    experts = lax.axis_size("expert")
    capacity = min(tok_rows, 2 * tok_rows * top_count // experts)
    slot_count = tok_rows * top_count
    buffer_rows = experts * capacity
    flat_ids = expert_ids.reshape(slot_count)
    onehot = (flat_ids[:, None] == jnp.arange(experts, dtype=jnp.int32)[None, :]).astype(jnp.int32)
    slot_rank = jnp.sum((jnp.cumsum(onehot, axis=0) - 1) * onehot, axis=1)
    position = flat_ids * capacity + slot_rank
    placing = (jnp.arange(buffer_rows, dtype=jnp.int32)[:, None] == position[None, :]).astype(
        jnp.bfloat16
    )
    token_map = placing.reshape(buffer_rows, tok_rows, top_count).sum(axis=2)
    x_send = jnp.dot(token_map, tokens, preferred_element_type=jnp.float32).astype(jnp.bfloat16)
    x_send = x_send.reshape(experts, capacity, model_width)
    cot_send = jnp.dot(token_map, cotangent, preferred_element_type=jnp.float32).astype(
        jnp.bfloat16
    )
    cot_send = cot_send.reshape(experts, capacity, model_width)
    gate_send = jnp.dot(
        placing, gate_weights.reshape(slot_count), preferred_element_type=jnp.float32
    )
    gate_send = gate_send.astype(jnp.bfloat16).reshape(experts, capacity)
    gate_mat = w_gate[0]
    up_mat = w_up[0]
    down_mat = w_down[0]
    x_recv = lax.all_to_all(x_send, "expert", split_axis=0, concat_axis=0, tiled=True)
    expert_rows = x_recv.reshape(buffer_rows, model_width)
    pre_gate, pre_up, gate_sigmoid, hidden, outputs = expert_forward(
        expert_rows, gate_mat, up_mat, down_mat
    )
    cot_recv, gate_recv = (
        lax.all_to_all(cot_send, "expert", split_axis=0, concat_axis=0, tiled=True),
        lax.all_to_all(gate_send, "expert", split_axis=0, concat_axis=0, tiled=True),
    )
    cot_rows = cot_recv.reshape(buffer_rows, model_width)
    gate_rows = gate_recv.reshape(buffer_rows).astype(jnp.float32)
    scaled = (gate_rows[:, None] * cot_rows.astype(jnp.float32)).astype(jnp.bfloat16)
    d_hidden = jnp.dot(scaled, down_mat, preferred_element_type=jnp.float32)
    d_pre_gate = (
        d_hidden * pre_up * gate_sigmoid * (1.0 + pre_gate * (1.0 - gate_sigmoid))
    ).astype(jnp.bfloat16)
    d_pre_up = (d_hidden * pre_gate * gate_sigmoid).astype(jnp.bfloat16)
    slot_grad = (
        jnp.dot(d_pre_gate, gate_mat, preferred_element_type=jnp.float32)
        + jnp.dot(d_pre_up, up_mat, preferred_element_type=jnp.float32)
    ).astype(jnp.bfloat16)
    pieces = []
    for operand, partner in ((d_pre_gate, expert_rows), (d_pre_up, expert_rows), (hidden, scaled)):
        pieces.append(rounded(contract_first(operand, partner)))
    summed = lax.psum_scatter(
        jnp.concatenate(pieces, axis=1).astype(jnp.bfloat16), "dp", scatter_dimension=0, tiled=True
    ).astype(jnp.float32)
    grad_gate = summed[:, :model_width].astype(jnp.bfloat16)[None]
    grad_up = summed[:, model_width : 2 * model_width].astype(jnp.bfloat16)[None]
    grad_down_t = summed[:, 2 * model_width :].astype(jnp.bfloat16)[None]
    slot_back = slot_grad.reshape(experts, capacity, model_width)
    out_send = outputs.reshape(experts, capacity, model_width)
    grad_back, out_back = (
        lax.all_to_all(slot_back, "expert", split_axis=0, concat_axis=0, tiled=True),
        lax.all_to_all(out_send, "expert", split_axis=0, concat_axis=0, tiled=True),
    )
    picked = out_back.reshape(buffer_rows, model_width)[position].astype(jnp.float32)
    picked = picked.reshape(tok_rows, top_count, model_width)
    gate_grad = jnp.sum(picked * cotangent.astype(jnp.float32)[:, None, :], axis=2).astype(
        jnp.bfloat16
    )
    gathered = grad_back.reshape(buffer_rows, model_width)[position].astype(jnp.float32)
    token_grad = gathered.reshape(tok_rows, top_count, model_width).sum(axis=1).astype(jnp.bfloat16)
    return (token_grad, gate_grad, grad_gate, grad_up, grad_down_t)


def stages_of(count, groups):
    core = groups
    bits = [1 << b for b in range(count.bit_length() - 1)]
    bits.remove(core)
    last = [bits[0], bits[1]]
    first = bits[:1:-1]
    steps = [[i ^ b for i in range(count)] for b in first]
    steps.append([i ^ (last[1] if i & core else last[0]) for i in range(count)])
    steps.append([i ^ (last[0] if i & core else last[1]) for i in range(count)])
    return steps, [i ^ core for i in range(count)]


def swap(value, partners):
    return lax.ppermute(value, BOTH, list(enumerate(partners)))


def gathered(value, steps):
    for partners in steps:
        value = jnp.concatenate([value, swap(value, partners)], axis=0)
    return value


def added(left, right):
    return (left.astype(jnp.float32) + right.astype(jnp.float32)).astype(jnp.bfloat16)


def scattered(value, steps):
    for partners in steps[::-1]:
        half = value.shape[0] // 2
        value = added(value[:half], swap(value[half:], partners))
    return value


def dense_body(tokens, expert_ids, gate_weights, cotangent, w_gate, w_up, w_down):
    model_width = tokens.shape[1]
    experts = lax.axis_size("expert")
    groups = lax.axis_size("dp")
    mine = lax.axis_index("expert")
    part = lax.axis_index("dp")
    hidden_units = w_gate.shape[1] // groups
    steps, core_swap = stages_of(experts * groups, groups)
    lanes = -(-experts // 128) * 128
    named = expert_ids[:, :, None] == jnp.arange(lanes, dtype=jnp.int32)[None, None, :]
    gate_table = jnp.sum(
        jnp.where(named, gate_weights.astype(jnp.float32)[:, :, None], 0.0), axis=1
    ).astype(jnp.bfloat16)
    x_own = gathered(jnp.concatenate([tokens, gate_table], axis=1), steps)
    x_other = swap(x_own, core_swap)
    cot_own = gathered(cotangent, steps)
    cot_other = swap(cot_own, core_swap)
    gate_mat = lax.dynamic_slice_in_dim(w_gate[0], part * hidden_units, hidden_units, 0)
    up_mat = lax.dynamic_slice_in_dim(w_up[0], part * hidden_units, hidden_units, 0)
    down_mat = lax.dynamic_slice_in_dim(w_down[0], part * hidden_units, hidden_units, 1)
    column = jnp.arange(lanes, dtype=jnp.int32)[None, :] == mine
    kept = []
    for x_rows, cot_rows in ((x_own, cot_own), (x_other, cot_other)):
        x_part = x_rows[:, :model_width]
        gate_rows = jnp.sum(
            jnp.where(column, x_rows[:, model_width:].astype(jnp.float32), 0.0),
            axis=1,
            keepdims=True,
        )
        pre_gate = contract_last(x_part, gate_mat)
        pre_up = contract_last(x_part, up_mat)
        gate_sigmoid = jax.nn.sigmoid(pre_gate)
        hidden = pre_gate * gate_sigmoid * pre_up
        raw = jnp.dot(cot_rows, down_mat, preferred_element_type=jnp.float32)
        score = jnp.sum(hidden * raw, axis=1, keepdims=True)
        d_hidden = gate_rows * raw
        d_pre_gate = (
            d_hidden * pre_up * gate_sigmoid * (1.0 + pre_gate * (1.0 - gate_sigmoid))
        ).astype(jnp.bfloat16)
        d_pre_up = (d_hidden * pre_gate * gate_sigmoid).astype(jnp.bfloat16)
        slot_grad = (
            jnp.dot(d_pre_gate, gate_mat, preferred_element_type=jnp.float32)
            + jnp.dot(d_pre_up, up_mat, preferred_element_type=jnp.float32)
        ).astype(jnp.bfloat16)
        scores = jnp.where(column, score, 0.0).astype(jnp.bfloat16)
        kept.append(
            (
                jnp.concatenate([slot_grad, scores], axis=1),
                d_pre_gate,
                d_pre_up,
                (gate_rows * hidden).astype(jnp.bfloat16),
            )
        )
    partial = added(kept[0][0], swap(kept[1][0], core_swap))
    result = scattered(partial, steps)
    token_grad = result[:, :model_width]
    gate_grad = jnp.sum(
        jnp.where(named, result[:, model_width:].astype(jnp.float32)[:, None, :], 0.0), axis=2
    ).astype(jnp.bfloat16)
    grads = []
    for place, (own, other) in (
        (1, (x_own, x_other)),
        (2, (x_own, x_other)),
        (3, (cot_own, cot_other)),
    ):
        total = contract_first(kept[0][place], own[:, :model_width]) + contract_first(
            kept[1][place], other[:, :model_width]
        )
        grads.append(total.astype(jnp.bfloat16)[None])
    return (token_grad, gate_grad, *grads)


def body(tokens, expert_ids, *rest):
    tok_rows, top_count = expert_ids.shape
    if 2 * tok_rows * top_count // lax.axis_size("expert") < tok_rows:
        return routed_body(tokens, expert_ids, *rest)
    return dense_body(tokens, expert_ids, *rest)


def solution(mesh):
    return jax.shard_map(
        body,
        mesh=mesh,
        in_specs=(
            P(("expert", "dp"), None),
            P(("expert", "dp"), None),
            P(("expert", "dp"), None),
            P(("expert", "dp"), None),
            P("expert", None, None),
            P("expert", None, None),
            P("expert", None, None),
        ),
        out_specs=(
            P(("expert", "dp"), None),
            P(("expert", "dp"), None),
            P("expert", "dp", None),
            P("expert", "dp", None),
            P("expert", "dp", None),
        ),
        check_vma=False,
    )
```

```python
import functools

import jax
import jax.numpy as jnp
from jax import lax
from jax.experimental import pallas as pl
from jax.experimental.pallas import tpu as pltpu
from jax.sharding import PartitionSpec as P

TILE = 256
BOTH = ("expert", "dp")


def contract_last(left, right):
    return lax.dot_general(
        left, right, (((1,), (1,)), ((), ())), preferred_element_type=jnp.float32
    )


def contract_first(left, right):
    return lax.dot_general(
        left, right, (((0,), (0,)), ((), ())), preferred_element_type=jnp.float32
    )


def rounded(value):
    return lax.optimization_barrier(value.astype(jnp.bfloat16)).astype(jnp.float32)


def expert_forward(expert_rows, gate_mat, up_mat, down_mat):
    pre_gate = contract_last(expert_rows, gate_mat)
    pre_up = contract_last(expert_rows, up_mat)
    gate_sigmoid = jax.nn.sigmoid(pre_gate)
    hidden = (pre_gate * gate_sigmoid * pre_up).astype(jnp.bfloat16)
    outputs = contract_last(hidden, down_mat).astype(jnp.bfloat16)
    return (pre_gate, pre_up, gate_sigmoid, hidden, outputs)


def routed_body(tokens, expert_ids, gate_weights, cotangent, w_gate, w_up, w_down):
    tok_rows, top_count = expert_ids.shape
    model_width = tokens.shape[1]
    experts = lax.axis_size("expert")
    capacity = min(tok_rows, 2 * tok_rows * top_count // experts)
    slot_count = tok_rows * top_count
    buffer_rows = experts * capacity
    flat_ids = expert_ids.reshape(slot_count)
    onehot = (flat_ids[:, None] == jnp.arange(experts, dtype=jnp.int32)[None, :]).astype(jnp.int32)
    slot_rank = jnp.sum((jnp.cumsum(onehot, axis=0) - 1) * onehot, axis=1)
    position = flat_ids * capacity + slot_rank
    placing = (jnp.arange(buffer_rows, dtype=jnp.int32)[:, None] == position[None, :]).astype(
        jnp.bfloat16
    )
    token_map = placing.reshape(buffer_rows, tok_rows, top_count).sum(axis=2)
    x_send = jnp.dot(token_map, tokens, preferred_element_type=jnp.float32).astype(jnp.bfloat16)
    x_send = x_send.reshape(experts, capacity, model_width)
    cot_send = jnp.dot(token_map, cotangent, preferred_element_type=jnp.float32).astype(
        jnp.bfloat16
    )
    cot_send = cot_send.reshape(experts, capacity, model_width)
    gate_send = jnp.dot(
        placing, gate_weights.reshape(slot_count), preferred_element_type=jnp.float32
    )
    gate_send = gate_send.astype(jnp.bfloat16).reshape(experts, capacity)
    gate_mat = w_gate[0]
    up_mat = w_up[0]
    down_mat = w_down[0]
    x_recv = lax.all_to_all(x_send, "expert", split_axis=0, concat_axis=0, tiled=True)
    expert_rows = x_recv.reshape(buffer_rows, model_width)
    pre_gate, pre_up, gate_sigmoid, hidden, outputs = expert_forward(
        expert_rows, gate_mat, up_mat, down_mat
    )
    cot_recv, gate_recv = (
        lax.all_to_all(cot_send, "expert", split_axis=0, concat_axis=0, tiled=True),
        lax.all_to_all(gate_send, "expert", split_axis=0, concat_axis=0, tiled=True),
    )
    cot_rows = cot_recv.reshape(buffer_rows, model_width)
    gate_rows = gate_recv.reshape(buffer_rows).astype(jnp.float32)
    scaled = (gate_rows[:, None] * cot_rows.astype(jnp.float32)).astype(jnp.bfloat16)
    d_hidden = jnp.dot(scaled, down_mat, preferred_element_type=jnp.float32)
    d_pre_gate = (
        d_hidden * pre_up * gate_sigmoid * (1.0 + pre_gate * (1.0 - gate_sigmoid))
    ).astype(jnp.bfloat16)
    d_pre_up = (d_hidden * pre_gate * gate_sigmoid).astype(jnp.bfloat16)
    slot_grad = (
        jnp.dot(d_pre_gate, gate_mat, preferred_element_type=jnp.float32)
        + jnp.dot(d_pre_up, up_mat, preferred_element_type=jnp.float32)
    ).astype(jnp.bfloat16)
    pieces = []
    for operand, partner in ((d_pre_gate, expert_rows), (d_pre_up, expert_rows), (hidden, scaled)):
        pieces.append(rounded(contract_first(operand, partner)))
    summed = lax.psum_scatter(
        jnp.concatenate(pieces, axis=1).astype(jnp.bfloat16), "dp", scatter_dimension=0, tiled=True
    ).astype(jnp.float32)
    grad_gate = summed[:, :model_width].astype(jnp.bfloat16)[None]
    grad_up = summed[:, model_width : 2 * model_width].astype(jnp.bfloat16)[None]
    grad_down_t = summed[:, 2 * model_width :].astype(jnp.bfloat16)[None]
    slot_back = slot_grad.reshape(experts, capacity, model_width)
    out_send = outputs.reshape(experts, capacity, model_width)
    grad_back, out_back = (
        lax.all_to_all(slot_back, "expert", split_axis=0, concat_axis=0, tiled=True),
        lax.all_to_all(out_send, "expert", split_axis=0, concat_axis=0, tiled=True),
    )
    picked = out_back.reshape(buffer_rows, model_width)[position].astype(jnp.float32)
    picked = picked.reshape(tok_rows, top_count, model_width)
    gate_grad = jnp.sum(picked * cotangent.astype(jnp.float32)[:, None, :], axis=2).astype(
        jnp.bfloat16
    )
    gathered = grad_back.reshape(buffer_rows, model_width)[position].astype(jnp.float32)
    token_grad = gathered.reshape(tok_rows, top_count, model_width).sum(axis=1).astype(jnp.bfloat16)
    return (token_grad, gate_grad, grad_gate, grad_up, grad_down_t)


def swap(value, flip):
    count = lax.axis_size(BOTH)
    return lax.ppermute(value, BOTH, [(i, i ^ flip) for i in range(count)])


def added(*terms):
    return sum(term.astype(jnp.float32) for term in terms).astype(jnp.bfloat16)


def tied(*values):
    return lax.optimization_barrier(values)


def kernel_params(flops, moved, transcendentals=0, megabytes=14):
    return {
        "compiler_params": pltpu.CompilerParams(vmem_limit_bytes=megabytes * 1024 * 1024),
        "cost_estimate": pl.CostEstimate(
            flops=flops, bytes_accessed=moved, transcendentals=transcendentals
        ),
    }


IN_HBM = pl.BlockSpec(memory_space=pl.ANY)
IN_VMEM = pl.BlockSpec(memory_space=pltpu.VMEM)
IN_SMEM = pl.BlockSpec(memory_space=pltpu.SMEM)


def kept(value):
    return pltpu.with_memory_space_constraint(value, pltpu.VMEM)


def left_out(value):
    return pltpu.with_memory_space_constraint(value, pltpu.HBM)


def fetched(pairs, sems):
    copies = [pltpu.make_async_copy(src, dst, sems.at[i]) for i, (src, dst) in enumerate(pairs)]
    for copy in copies:
        copy.start()
    return copies


def placed(pieces, target):
    pairs, first = [], 0
    for piece in pieces:
        pairs.append((piece, target.at[pl.ds(first, piece.shape[0])]))
        first += piece.shape[0]
    return pairs


def forward_kernel(*refs):
    pieces, weight_refs, weight_outs, sems = refs[:4], refs[4:7], refs[7:10], refs[-1]
    rows_out, slope_out, swish_out, hidden_out = refs[10:14]
    units = slope_out.shape[1]
    pairs = placed(pieces, rows_out)
    for start in range(0, units, TILE):
        for i in range(2):
            rows = pl.ds(start, TILE)
            pairs.append((weight_refs[i].at[0, rows], weight_outs[i].at[rows]))
    half = weight_outs[2].shape[0] // 2
    for i in range(2):
        rows = pl.ds(i * half, half)
        pairs.append((weight_refs[2].at[0, rows], weight_outs[2].at[rows]))
    copies = fetched(pairs, sems)
    for copy in copies[:4]:
        copy.wait()
    for step, start in enumerate(range(0, units, TILE)):
        for copy in copies[4 + 2 * step : 6 + 2 * step]:
            copy.wait()
        rows = rows_out[...]
        chunk = slice(start, start + TILE)
        pre_gate = contract_last(rows, weight_outs[0][chunk])
        pre_up = contract_last(rows, weight_outs[1][chunk])
        gate_sigmoid = jax.nn.sigmoid(pre_gate)
        swish = pre_gate * gate_sigmoid
        slope_out[:, chunk] = pre_up * gate_sigmoid * (1.0 + pre_gate * (1.0 - gate_sigmoid))
        swish_out[:, chunk] = swish
        hidden_out[:, chunk] = swish * pre_up
    for copy in copies[-2:]:
        copy.wait()


def forward(pieces, weights):
    _, units, width = weights[0].shape
    rows = sum(piece.shape[0] for piece in pieces)
    outs = [pltpu.VMEM((rows, units), jnp.float32)] * 3
    for shape in ((rows, width), (width, units), (units, width), (units, width)):
        outs.insert(0, pltpu.VMEM(shape, jnp.bfloat16))
    return pl.pallas_call(
        forward_kernel,
        in_specs=[IN_HBM] * 7,
        out_specs=[IN_VMEM] * 7,
        out_shape=outs,
        scratch_shapes=[pltpu.SemaphoreType.DMA((6 + 2 * (units // TILE),))],
        **kernel_params(4 * rows * units * width, 2 * rows * width, rows * units),
    )(*[left_out(value) for value in (*pieces, *weights)])


def backward_kernel(
    which,
    place_ref,
    own_ref,
    other_ref,
    slope_ref,
    swish_ref,
    hidden_ref,
    gate_ref,
    up_ref,
    down_ref,
    _,
    own_out,
    other_out,
    rows_out,
    lefts_out,
    token_out,
    sems,
):
    width, units = down_ref.shape
    half = own_ref.shape[0]
    lanes = own_ref.shape[1] - width
    copies = fetched(placed((own_ref, other_ref), rows_out), sems)
    token_out[...] = jnp.zeros_like(token_out)
    for copy in copies:
        copy.wait()
    saved = pl.ds(which * 2 * half, 2 * half)
    column = lax.broadcasted_iota(jnp.int32, (2 * half, lanes), 1) == place_ref[0]
    table = rows_out[:, width:].astype(jnp.float32)
    gates = jnp.sum(jnp.where(column, table, 0.0), axis=1, keepdims=True)
    score = jnp.zeros((2 * half, 1), jnp.float32)
    for start in range(0, units, TILE):
        chunk = slice(start, start + TILE)
        raw = jnp.dot(
            rows_out[:, :width], down_ref[:, chunk], preferred_element_type=jnp.float32
        )
        hidden = hidden_ref[saved, chunk]
        score += jnp.sum(hidden * raw, axis=1, keepdims=True)
        d_hidden = gates * raw
        lefts_out[:, chunk] = (d_hidden * slope_ref[saved, chunk]).astype(jnp.bfloat16)
        lefts_out[:, units + start : units + start + TILE] = (
            d_hidden * swish_ref[saved, chunk]
        ).astype(jnp.bfloat16)
        lefts_out[:, 2 * units + start : 2 * units + start + TILE] = (gates * hidden).astype(
            jnp.bfloat16
        )
    scores = jnp.where(column, score, 0.0).astype(jnp.bfloat16)
    own_out[:, width:] = scores[:half]
    other_out[:, width:] = scores[half:]
    for start in range(0, width, 2 * TILE):
        chunk = slice(start, start + 2 * TILE)
        total = (
            jnp.dot(lefts_out[:, :units], gate_ref[:, chunk], preferred_element_type=jnp.float32)
            + jnp.dot(
                lefts_out[:, units : 2 * units],
                up_ref[:, chunk],
                preferred_element_type=jnp.float32,
            )
        ).astype(jnp.bfloat16)
        own_out[:, chunk] = total[:half]
        other_out[:, chunk] = total[half:]


def backward(place, own, other, saved, which, weights, after):
    units, width = weights[0].shape
    half, packed = own.shape
    rows = 2 * half
    return pl.pallas_call(
        functools.partial(backward_kernel, which),
        in_specs=[IN_SMEM] + [IN_HBM] * 2 + [IN_VMEM] * 6 + [IN_HBM],
        out_specs=[IN_VMEM] * 5,
        out_shape=[
            jax.ShapeDtypeStruct((half, packed), jnp.bfloat16),
            jax.ShapeDtypeStruct((half, packed), jnp.bfloat16),
            pltpu.VMEM((rows, packed), jnp.bfloat16),
            pltpu.VMEM((rows, 3 * units), jnp.bfloat16),
            jax.ShapeDtypeStruct((8, 128), jnp.float32),
        ],
        scratch_shapes=[pltpu.SemaphoreType.DMA((2,))],
        **kernel_params(0, 0),
    )(place, own, other, *[kept(value) for value in (*saved, *weights)], after)


def own_gradient_kernel(place_ref, column_ref, near_ref, x_ref, column_cot, near_cot, *refs):
    outs, token_out, lefts = refs[:3], refs[3], refs[4]
    share, tile = outs[0].shape
    units = column_ref.shape[1] // 3

    @pl.when(pl.program_id(0) == 0)
    def _():
        token_out[...] = jnp.zeros_like(token_out)
        start = pl.multiple_of(place_ref[1] * share, 128)
        for i in range(3):
            lefts[i] = jnp.concatenate(
                [ref[:, pl.ds(start + i * units, share)] for ref in (column_ref, near_ref)], axis=0
            ).T

    chunk = pl.ds(pl.multiple_of(pl.program_id(0) * tile, tile), tile)
    cot_rows = jnp.concatenate([column_cot[:, chunk], near_cot[:, chunk]], axis=0)
    for i, rows in enumerate((x_ref[:, chunk], x_ref[:, chunk], cot_rows)):
        outs[i][...] = jnp.dot(lefts[i], rows, preferred_element_type=jnp.float32).astype(
            jnp.bfloat16
        )


def own_gradients(place, lefts, x_rows, cot_rows, share):
    rows, width = x_rows.shape
    tile = 2 * TILE
    return pl.pallas_call(
        own_gradient_kernel,
        grid=(width // tile,),
        in_specs=[IN_SMEM] + [IN_VMEM] * 5,
        out_specs=[pl.BlockSpec((share, tile), lambda i: (0, i))] * 3
        + [pl.BlockSpec((8, 128), lambda i: (0, 0))],
        out_shape=[jax.ShapeDtypeStruct((share, width), jnp.bfloat16)] * 3
        + [jax.ShapeDtypeStruct((8, 128), jnp.float32)],
        scratch_shapes=[pltpu.VMEM((3, share, rows), jnp.bfloat16)],
        **kernel_params(6 * rows * share * width, 6 * share * width),
    )(place, *[kept(value) for value in (*lefts, x_rows, *cot_rows)])


def whole_gradient_kernel(place_ref, *refs):
    x_refs, cot_refs, weight_refs, own_refs = refs[:6], refs[6:14], refs[14:17], refs[17:20]
    outs, (rows, cot, gate_ref, up_ref, down_ref, lefts, sems) = refs[21:24], refs[24:]
    share, tile = outs[0].shape[1:]
    width = rows.shape[1]

    @pl.when(pl.program_id(0) == 0)
    def _():
        own = pl.ds(pl.multiple_of(place_ref[1] * share, 128), share)
        copies = fetched(
            placed(x_refs, rows)
            + [(weight_refs[0].at[0, own], gate_ref), (weight_refs[1].at[0, own], up_ref)]
            + placed(cot_refs, cot)
            + [(weight_refs[2].at[0, :, own], down_ref)],
            sems,
        )
        for copy in copies[:8]:
            copy.wait()
        pre_gate = contract_last(gate_ref[...], rows[...])
        pre_up = contract_last(up_ref[...], rows[...])
        gate_sigmoid = jax.nn.sigmoid(pre_gate)
        swish = pre_gate * gate_sigmoid
        for copy in copies[8:]:
            copy.wait()
        table = cot[:, width:]
        pick = (lax.broadcasted_iota(jnp.int32, (16, table.shape[1]), 1) == place_ref[0]).astype(
            jnp.bfloat16
        )
        gates = contract_last(pick, table)[:1]
        raw = jnp.dot(cot[:, :width], down_ref[...], preferred_element_type=jnp.float32).T
        d_hidden = gates * raw
        lefts[0] = (
            d_hidden * pre_up * gate_sigmoid * (1.0 + pre_gate * (1.0 - gate_sigmoid))
        ).astype(jnp.bfloat16)
        lefts[1] = (d_hidden * swish).astype(jnp.bfloat16)
        lefts[2] = (gates * (swish * pre_up)).astype(jnp.bfloat16)

    first = pl.multiple_of(pl.program_id(0) * tile, tile)
    for i in range(3):
        right = rows if i < 2 else cot
        away = jnp.dot(lefts[i], right[:, pl.ds(first, tile)], preferred_element_type=jnp.float32)
        outs[i][0] = (own_refs[i][...].astype(jnp.float32) + away).astype(jnp.bfloat16)


def whole_gradients(place, x_rows, cot_rows, weights, own, after):
    share, width = own[0].shape
    tile = 2 * TILE
    rows = sum(piece.shape[0] for piece in x_rows)
    half = pltpu.VMEM((share, width), jnp.bfloat16)
    return pl.pallas_call(
        whole_gradient_kernel,
        grid=(width // tile,),
        in_specs=[IN_SMEM]
        + [IN_HBM] * 17
        + [pl.BlockSpec((share, tile), lambda i: (0, i))] * 3
        + [IN_HBM],
        out_specs=[pl.BlockSpec((1, share, tile), lambda i: (0, 0, i))] * 3,
        out_shape=[jax.ShapeDtypeStruct((1, share, width), jnp.bfloat16)] * 3,
        scratch_shapes=[
            pltpu.VMEM((rows, width), jnp.bfloat16),
            pltpu.VMEM((rows, cot_rows[0].shape[1]), jnp.bfloat16),
            half,
            half,
            pltpu.VMEM((width, share), jnp.bfloat16),
            pltpu.VMEM((3, share, rows), jnp.bfloat16),
            pltpu.SemaphoreType.DMA((17,)),
        ],
        **kernel_params(
            12 * rows * share * width, 4 * rows * width + 12 * share * width, rows * share, 32
        ),
    )(place, *[left_out(value) for value in (*x_rows, *cot_rows, *weights, *own)], after)


def dense_body(tokens, expert_ids, gate_weights, cotangent, w_gate, w_up, w_down):
    model_width = tokens.shape[1]
    experts = lax.axis_size("expert")
    groups = lax.axis_size("dp")
    share = w_gate.shape[1] // groups
    place = jnp.stack([lax.axis_index("expert"), lax.axis_index("dp")]).astype(jnp.int32)
    group, core, near, low, high = 1, 2, 4, 8, 16
    lanes = -(-experts // 128) * 128
    named = expert_ids[:, :, None] == jnp.arange(lanes, dtype=jnp.int32)[None, None, :]
    gate_table = jnp.sum(
        jnp.where(named, gate_weights.astype(jnp.float32)[:, :, None], 0.0), axis=1
    ).astype(jnp.bfloat16)

    def column_of(value):
        return [swap(value, high), swap(value, low | high), swap(value, low)]

    weights = (w_gate, w_up, w_down)
    packed = jnp.concatenate([cotangent, gate_table], axis=1)
    x_mine_away, cot_mine_away = swap(tokens, group), swap(packed, group)
    packed, x_mine_away, cot_mine_away, *x_far = tied(
        packed, x_mine_away, cot_mine_away, *column_of(tokens)
    )
    x_far = jnp.concatenate(x_far, axis=0)
    x_column = jnp.concatenate([tokens, x_far], axis=0)
    x_near = swap(x_column, near)
    x_far_away, x_near_away = swap(x_far, group), swap(x_near, group)
    *cot_far, x_far_away = tied(*column_of(packed), x_far_away)
    x_far_other = swap(x_far_away, core)
    cot_column = jnp.concatenate([packed, *cot_far], axis=0)
    cot_first_away = swap(cot_far[0], group)
    cot_near = swap(cot_column, near)
    *kept_weights, x_rows, slope, swish, hidden = forward(
        [x_column, swap(x_column, core), x_near, swap(x_near, core)], weights
    )
    saved = (slope, swish, hidden)
    own_part, other_part, column_cot, column_lefts, token = backward(
        place, cot_column, swap(cot_column, core), saved, 0, kept_weights, place
    )
    column_partial = added(own_part, swap(other_part, core))
    cot_near, token, x_near_away, x_far_other = tied(cot_near, token, x_near_away, x_far_other)
    x_near_other = swap(x_near_away, core)
    x_mine_other, cot_mine_other = swap(x_mine_away, core), swap(cot_mine_away, core)
    cot_second_away = swap(jnp.concatenate(cot_far[1:], axis=0), group)
    cot_near_away = swap(cot_near, group)
    own_part, other_part, near_cot, near_lefts, _ = backward(
        place, cot_near, swap(cot_near, core), saved, 1, kept_weights, token
    )
    other_part, cot_second_away, x_near_other, x_mine_other, cot_mine_other = tied(
        other_part, cot_second_away, x_near_other, x_mine_other, cot_mine_other
    )
    cot_second_other = swap(cot_second_away, core)
    near_partial = added(own_part, swap(other_part, core))
    partial = added(column_partial, swap(near_partial, near))
    *own, token = own_gradients(
        place, [column_lefts, near_lefts], x_rows, [column_cot, near_cot], share
    )
    partial, cot_first_away, cot_near_away, cot_second_other, token = tied(
        partial, cot_first_away, cot_near_away, cot_second_other, token
    )
    x_away = [x_mine_away, x_far_away, x_near_away, x_mine_other, x_far_other, x_near_other]
    cot_away = [cot_mine_away, cot_first_away, cot_second_away, cot_near_away]
    cot_away += [cot_mine_other, swap(cot_first_away, core), cot_second_other]
    cot_away += [swap(cot_near_away, core)]
    grads = list(whole_gradients(place, x_away, cot_away, weights, own, token))
    block = partial.shape[0] // 4
    parts = [
        partial[:block],
        swap(partial[block : 2 * block], high),
        swap(partial[2 * block : 3 * block], low | high),
        swap(partial[3 * block :], low),
    ]
    *parts, grads[0] = tied(*parts, grads[0])
    result = added(*parts)
    token_grad = result[:, :model_width]
    gate_grad = jnp.sum(
        jnp.where(named, result[:, model_width:].astype(jnp.float32)[:, None, :], 0.0), axis=2
    ).astype(jnp.bfloat16)
    return (token_grad, gate_grad, *grads)


def body(tokens, expert_ids, *rest):
    tok_rows, top_count = expert_ids.shape
    if 2 * tok_rows * top_count // lax.axis_size("expert") < tok_rows:
        return routed_body(tokens, expert_ids, *rest)
    return dense_body(tokens, expert_ids, *rest)


def solution(mesh):
    return jax.shard_map(
        body,
        mesh=mesh,
        in_specs=(
            P(("expert", "dp"), None),
            P(("expert", "dp"), None),
            P(("expert", "dp"), None),
            P(("expert", "dp"), None),
            P("expert", None, None),
            P("expert", None, None),
            P("expert", None, None),
        ),
        out_specs=(
            P(("expert", "dp"), None),
            P(("expert", "dp"), None),
            P("expert", "dp", None),
            P("expert", "dp", None),
            P("expert", "dp", None),
        ),
        check_vma=False,
    )
```

```python
import functools

import jax
import jax.numpy as jnp
from jax import lax
from jax.experimental import pallas as pl
from jax.experimental.pallas import tpu as pltpu
from jax.sharding import PartitionSpec as P

TILE = 256
BOTH = ("expert", "dp")


def contract_last(left, right):
    return lax.dot_general(
        left, right, (((1,), (1,)), ((), ())), preferred_element_type=jnp.float32
    )


def contract_first(left, right):
    return lax.dot_general(
        left, right, (((0,), (0,)), ((), ())), preferred_element_type=jnp.float32
    )


def rounded(value):
    return lax.optimization_barrier(value.astype(jnp.bfloat16)).astype(jnp.float32)


def expert_forward(expert_rows, gate_mat, up_mat, down_mat):
    pre_gate = contract_last(expert_rows, gate_mat)
    pre_up = contract_last(expert_rows, up_mat)
    gate_sigmoid = jax.nn.sigmoid(pre_gate)
    hidden = (pre_gate * gate_sigmoid * pre_up).astype(jnp.bfloat16)
    outputs = contract_last(hidden, down_mat).astype(jnp.bfloat16)
    return (pre_gate, pre_up, gate_sigmoid, hidden, outputs)


def routed_body(tokens, expert_ids, gate_weights, cotangent, w_gate, w_up, w_down):
    tok_rows, top_count = expert_ids.shape
    model_width = tokens.shape[1]
    experts = lax.axis_size("expert")
    capacity = min(tok_rows, 2 * tok_rows * top_count // experts)
    slot_count = tok_rows * top_count
    buffer_rows = experts * capacity
    flat_ids = expert_ids.reshape(slot_count)
    onehot = (flat_ids[:, None] == jnp.arange(experts, dtype=jnp.int32)[None, :]).astype(jnp.int32)
    slot_rank = jnp.sum((jnp.cumsum(onehot, axis=0) - 1) * onehot, axis=1)
    position = flat_ids * capacity + slot_rank
    placing = (jnp.arange(buffer_rows, dtype=jnp.int32)[:, None] == position[None, :]).astype(
        jnp.bfloat16
    )
    token_map = placing.reshape(buffer_rows, tok_rows, top_count).sum(axis=2)
    x_send = jnp.dot(token_map, tokens, preferred_element_type=jnp.float32).astype(jnp.bfloat16)
    x_send = x_send.reshape(experts, capacity, model_width)
    cot_send = jnp.dot(token_map, cotangent, preferred_element_type=jnp.float32).astype(
        jnp.bfloat16
    )
    cot_send = cot_send.reshape(experts, capacity, model_width)
    gate_send = jnp.dot(
        placing, gate_weights.reshape(slot_count), preferred_element_type=jnp.float32
    )
    gate_send = gate_send.astype(jnp.bfloat16).reshape(experts, capacity)
    gate_mat = w_gate[0]
    up_mat = w_up[0]
    down_mat = w_down[0]
    x_recv = lax.all_to_all(x_send, "expert", split_axis=0, concat_axis=0, tiled=True)
    expert_rows = x_recv.reshape(buffer_rows, model_width)
    pre_gate, pre_up, gate_sigmoid, hidden, outputs = expert_forward(
        expert_rows, gate_mat, up_mat, down_mat
    )
    cot_recv, gate_recv = (
        lax.all_to_all(cot_send, "expert", split_axis=0, concat_axis=0, tiled=True),
        lax.all_to_all(gate_send, "expert", split_axis=0, concat_axis=0, tiled=True),
    )
    cot_rows = cot_recv.reshape(buffer_rows, model_width)
    gate_rows = gate_recv.reshape(buffer_rows).astype(jnp.float32)
    scaled = (gate_rows[:, None] * cot_rows.astype(jnp.float32)).astype(jnp.bfloat16)
    d_hidden = jnp.dot(scaled, down_mat, preferred_element_type=jnp.float32)
    d_pre_gate = (
        d_hidden * pre_up * gate_sigmoid * (1.0 + pre_gate * (1.0 - gate_sigmoid))
    ).astype(jnp.bfloat16)
    d_pre_up = (d_hidden * pre_gate * gate_sigmoid).astype(jnp.bfloat16)
    slot_grad = (
        jnp.dot(d_pre_gate, gate_mat, preferred_element_type=jnp.float32)
        + jnp.dot(d_pre_up, up_mat, preferred_element_type=jnp.float32)
    ).astype(jnp.bfloat16)
    pieces = []
    for operand, partner in ((d_pre_gate, expert_rows), (d_pre_up, expert_rows), (hidden, scaled)):
        pieces.append(rounded(contract_first(operand, partner)))
    summed = lax.psum_scatter(
        jnp.concatenate(pieces, axis=1).astype(jnp.bfloat16), "dp", scatter_dimension=0, tiled=True
    ).astype(jnp.float32)
    grad_gate = summed[:, :model_width].astype(jnp.bfloat16)[None]
    grad_up = summed[:, model_width : 2 * model_width].astype(jnp.bfloat16)[None]
    grad_down_t = summed[:, 2 * model_width :].astype(jnp.bfloat16)[None]
    slot_back = slot_grad.reshape(experts, capacity, model_width)
    out_send = outputs.reshape(experts, capacity, model_width)
    grad_back, out_back = (
        lax.all_to_all(slot_back, "expert", split_axis=0, concat_axis=0, tiled=True),
        lax.all_to_all(out_send, "expert", split_axis=0, concat_axis=0, tiled=True),
    )
    picked = out_back.reshape(buffer_rows, model_width)[position].astype(jnp.float32)
    picked = picked.reshape(tok_rows, top_count, model_width)
    gate_grad = jnp.sum(picked * cotangent.astype(jnp.float32)[:, None, :], axis=2).astype(
        jnp.bfloat16
    )
    gathered = grad_back.reshape(buffer_rows, model_width)[position].astype(jnp.float32)
    token_grad = gathered.reshape(tok_rows, top_count, model_width).sum(axis=1).astype(jnp.bfloat16)
    return (token_grad, gate_grad, grad_gate, grad_up, grad_down_t)


def swap(value, flip):
    count = lax.axis_size(BOTH)
    return lax.ppermute(value, BOTH, [(i, i ^ flip) for i in range(count)])


def added(*terms):
    return sum(term.astype(jnp.float32) for term in terms).astype(jnp.bfloat16)


def tied(*values):
    return lax.optimization_barrier(values)


def kernel_params(flops, moved, transcendentals=0, megabytes=14):
    return {
        "compiler_params": pltpu.CompilerParams(vmem_limit_bytes=megabytes * 1024 * 1024),
        "cost_estimate": pl.CostEstimate(
            flops=flops, bytes_accessed=moved, transcendentals=transcendentals
        ),
    }


IN_HBM = pl.BlockSpec(memory_space=pl.ANY)
IN_VMEM = pl.BlockSpec(memory_space=pltpu.VMEM)
IN_SMEM = pl.BlockSpec(memory_space=pltpu.SMEM)


def kept(value):
    return pltpu.with_memory_space_constraint(value, pltpu.VMEM)


def left_out(value):
    return pltpu.with_memory_space_constraint(value, pltpu.HBM)


def fetched(pairs, sems):
    copies = [pltpu.make_async_copy(src, dst, sems.at[i]) for i, (src, dst) in enumerate(pairs)]
    for copy in copies:
        copy.start()
    return copies


def placed(pieces, target):
    pairs, first = [], 0
    for piece in pieces:
        pairs.append((piece, target.at[pl.ds(first, piece.shape[0])]))
        first += piece.shape[0]
    return pairs


def forward_kernel(*refs):
    pieces, weight_refs, weight_outs, sems = refs[:4], refs[4:7], refs[7:10], refs[-1]
    rows_out, slope_out, swish_out, hidden_out = refs[10:14]
    units = slope_out.shape[1]
    pairs = placed(pieces, rows_out)
    for start in range(0, units, TILE):
        for i in range(2):
            rows = pl.ds(start, TILE)
            pairs.append((weight_refs[i].at[0, rows], weight_outs[i].at[rows]))
    half = weight_outs[2].shape[0] // 2
    for i in range(2):
        rows = pl.ds(i * half, half)
        pairs.append((weight_refs[2].at[0, rows], weight_outs[2].at[rows]))
    copies = fetched(pairs, sems)
    for copy in copies[:4]:
        copy.wait()
    for step, start in enumerate(range(0, units, TILE)):
        for copy in copies[4 + 2 * step : 6 + 2 * step]:
            copy.wait()
        rows = rows_out[...]
        chunk = slice(start, start + TILE)
        pre_gate = contract_last(rows, weight_outs[0][chunk])
        pre_up = contract_last(rows, weight_outs[1][chunk])
        gate_sigmoid = jax.nn.sigmoid(pre_gate)
        swish = pre_gate * gate_sigmoid
        slope_out[:, chunk] = pre_up * gate_sigmoid * (1.0 + pre_gate * (1.0 - gate_sigmoid))
        swish_out[:, chunk] = swish
        hidden_out[:, chunk] = swish * pre_up
    for copy in copies[-2:]:
        copy.wait()


def forward(pieces, weights):
    _, units, width = weights[0].shape
    rows = sum(piece.shape[0] for piece in pieces)
    outs = [pltpu.VMEM((rows, units), jnp.float32)] * 3
    for shape in ((rows, width), (width, units), (units, width), (units, width)):
        outs.insert(0, pltpu.VMEM(shape, jnp.bfloat16))
    return pl.pallas_call(
        forward_kernel,
        in_specs=[IN_HBM] * 7,
        out_specs=[IN_VMEM] * 7,
        out_shape=outs,
        scratch_shapes=[pltpu.SemaphoreType.DMA((6 + 2 * (units // TILE),))],
        **kernel_params(4 * rows * units * width, 2 * rows * width, rows * units),
    )(*[left_out(value) for value in (*pieces, *weights)])


def backward_kernel(
    which,
    place_ref,
    own_ref,
    other_ref,
    slope_ref,
    swish_ref,
    hidden_ref,
    gate_ref,
    up_ref,
    down_ref,
    _,
    own_out,
    other_out,
    rows_out,
    lefts_out,
    token_out,
    sems,
):
    width, units = down_ref.shape
    half = own_ref.shape[0]
    lanes = own_ref.shape[1] - width
    copies = fetched(placed((own_ref, other_ref), rows_out), sems)
    token_out[...] = jnp.zeros_like(token_out)
    for copy in copies:
        copy.wait()
    saved = pl.ds(which * 2 * half, 2 * half)
    column = lax.broadcasted_iota(jnp.int32, (2 * half, lanes), 1) == place_ref[0]
    table = rows_out[:, width:].astype(jnp.float32)
    gates = jnp.sum(jnp.where(column, table, 0.0), axis=1, keepdims=True)
    score = jnp.zeros((2 * half, 1), jnp.float32)
    for start in range(0, units, TILE):
        chunk = slice(start, start + TILE)
        raw = jnp.dot(
            rows_out[:, :width], down_ref[:, chunk], preferred_element_type=jnp.float32
        )
        hidden = hidden_ref[saved, chunk]
        score += jnp.sum(hidden * raw, axis=1, keepdims=True)
        d_hidden = gates * raw
        lefts_out[:, chunk] = (d_hidden * slope_ref[saved, chunk]).astype(jnp.bfloat16)
        lefts_out[:, units + start : units + start + TILE] = (
            d_hidden * swish_ref[saved, chunk]
        ).astype(jnp.bfloat16)
        lefts_out[:, 2 * units + start : 2 * units + start + TILE] = (gates * hidden).astype(
            jnp.bfloat16
        )
    scores = jnp.where(column, score, 0.0).astype(jnp.bfloat16)
    own_out[:, width:] = scores[:half]
    other_out[:, width:] = scores[half:]
    for start in range(0, width, 2 * TILE):
        chunk = slice(start, start + 2 * TILE)
        total = (
            jnp.dot(lefts_out[:, :units], gate_ref[:, chunk], preferred_element_type=jnp.float32)
            + jnp.dot(
                lefts_out[:, units : 2 * units],
                up_ref[:, chunk],
                preferred_element_type=jnp.float32,
            )
        ).astype(jnp.bfloat16)
        own_out[:, chunk] = total[:half]
        other_out[:, chunk] = total[half:]


def backward(place, own, other, saved, which, weights, after):
    units, width = weights[0].shape
    half, packed = own.shape
    rows = 2 * half
    return pl.pallas_call(
        functools.partial(backward_kernel, which),
        in_specs=[IN_SMEM] + [IN_HBM] * 2 + [IN_VMEM] * 6 + [IN_HBM],
        out_specs=[IN_VMEM] * 5,
        out_shape=[
            jax.ShapeDtypeStruct((half, packed), jnp.bfloat16),
            jax.ShapeDtypeStruct((half, packed), jnp.bfloat16),
            pltpu.VMEM((rows, packed), jnp.bfloat16),
            pltpu.VMEM((rows, 3 * units), jnp.bfloat16),
            jax.ShapeDtypeStruct((8, 128), jnp.float32),
        ],
        scratch_shapes=[pltpu.SemaphoreType.DMA((2,))],
        **kernel_params(0, 0),
    )(place, own, other, *[kept(value) for value in (*saved, *weights)], after)


def own_gradient_kernel(place_ref, column_ref, near_ref, x_ref, column_cot, near_cot, *refs):
    outs, token_out, lefts = refs[:3], refs[3], refs[4]
    share, tile = outs[0].shape
    units = column_ref.shape[1] // 3

    @pl.when(pl.program_id(0) == 0)
    def _():
        token_out[...] = jnp.zeros_like(token_out)
        start = pl.multiple_of(place_ref[1] * share, 128)
        for i in range(3):
            lefts[i] = jnp.concatenate(
                [ref[:, pl.ds(start + i * units, share)] for ref in (column_ref, near_ref)], axis=0
            ).T

    chunk = pl.ds(pl.multiple_of(pl.program_id(0) * tile, tile), tile)
    cot_rows = jnp.concatenate([column_cot[:, chunk], near_cot[:, chunk]], axis=0)
    for i, rows in enumerate((x_ref[:, chunk], x_ref[:, chunk], cot_rows)):
        outs[i][...] = jnp.dot(lefts[i], rows, preferred_element_type=jnp.float32).astype(
            jnp.bfloat16
        )


def own_gradients(place, lefts, x_rows, cot_rows, share):
    rows, width = x_rows.shape
    tile = 2 * TILE
    return pl.pallas_call(
        own_gradient_kernel,
        grid=(width // tile,),
        in_specs=[IN_SMEM] + [IN_VMEM] * 5,
        out_specs=[pl.BlockSpec((share, tile), lambda i: (0, i))] * 3
        + [pl.BlockSpec((8, 128), lambda i: (0, 0))],
        out_shape=[jax.ShapeDtypeStruct((share, width), jnp.bfloat16)] * 3
        + [jax.ShapeDtypeStruct((8, 128), jnp.float32)],
        scratch_shapes=[pltpu.VMEM((3, share, rows), jnp.bfloat16)],
        **kernel_params(6 * rows * share * width, 6 * share * width),
    )(place, *[kept(value) for value in (*lefts, x_rows, *cot_rows)])


def away_forward_kernel(place_ref, *refs):
    x_refs, weight_refs = refs[:4], refs[4:6]
    slope_out, swish_out, hidden_out, token_out, rows, gate_ref, up_ref, sems = refs[7:]
    share = gate_ref.shape[0]
    own = pl.ds(pl.multiple_of(place_ref[1] * share, 128), share)
    copies = fetched(
        placed(x_refs, rows)
        + [(weight_refs[0].at[0, own], gate_ref), (weight_refs[1].at[0, own], up_ref)],
        sems,
    )
    token_out[...] = jnp.zeros_like(token_out)
    for copy in copies[:5]:
        copy.wait()
    pre_gate = contract_last(gate_ref[...], rows[...])
    copies[5].wait()
    pre_up = contract_last(up_ref[...], rows[...])
    gate_sigmoid = jax.nn.sigmoid(pre_gate)
    swish = pre_gate * gate_sigmoid
    slope_out[...] = pre_up * gate_sigmoid * (1.0 + pre_gate * (1.0 - gate_sigmoid))
    swish_out[...] = swish
    hidden_out[...] = swish * pre_up


def away_forward(place, x_rows, weights, share, after):
    width = x_rows[0].shape[1]
    rows = sum(piece.shape[0] for piece in x_rows)
    half = pltpu.VMEM((share, width), jnp.bfloat16)
    return pl.pallas_call(
        away_forward_kernel,
        in_specs=[IN_SMEM] + [IN_HBM] * 7,
        out_specs=[IN_VMEM] * 4,
        out_shape=[jax.ShapeDtypeStruct((share, rows), jnp.float32)] * 3
        + [jax.ShapeDtypeStruct((8, 128), jnp.float32)],
        scratch_shapes=[
            pltpu.VMEM((rows, width), jnp.bfloat16),
            half,
            half,
            pltpu.SemaphoreType.DMA((6,)),
        ],
        **kernel_params(4 * rows * share * width, 2 * rows * width, rows * share, 20),
    )(place, *[left_out(value) for value in (*x_rows, *weights)], after)


def whole_gradient_kernel(place_ref, *refs):
    cot_refs, down_ref, saved_refs, x_refs = refs[:4], refs[4], refs[5:8], refs[8:12]
    own_refs, outs = refs[12:15], refs[16:19]
    rows, cot, down, slope, swish, hidden, lefts, sems = refs[19:]
    share, tile = outs[0].shape[1:]
    width = rows.shape[1]

    @pl.when(pl.program_id(0) == 0)
    def _():
        own = pl.ds(pl.multiple_of(place_ref[1] * share, 128), share)
        copies = fetched(
            placed(cot_refs, cot)
            + [(down_ref.at[0, :, own], down)]
            + list(zip(saved_refs, (slope, swish, hidden)))
            + placed(x_refs, rows),
            sems,
        )
        for copy in copies[:5]:
            copy.wait()
        table = cot[:, width:]
        pick = (lax.broadcasted_iota(jnp.int32, (16, table.shape[1]), 1) == place_ref[0]).astype(
            jnp.bfloat16
        )
        gates = contract_last(pick, table)[:1]
        raw = jnp.dot(cot[:, :width], down[...], preferred_element_type=jnp.float32).T
        d_hidden = gates * raw
        for copy in copies[5:8]:
            copy.wait()
        lefts[0] = (d_hidden * slope[...]).astype(jnp.bfloat16)
        lefts[1] = (d_hidden * swish[...]).astype(jnp.bfloat16)
        lefts[2] = (gates * hidden[...]).astype(jnp.bfloat16)
        for copy in copies[8:]:
            copy.wait()

    first = pl.multiple_of(pl.program_id(0) * tile, tile)
    for i in range(3):
        right = rows if i < 2 else cot
        away = jnp.dot(lefts[i], right[:, pl.ds(first, tile)], preferred_element_type=jnp.float32)
        outs[i][0] = (own_refs[i][...].astype(jnp.float32) + away).astype(jnp.bfloat16)


def whole_gradients(place, cot_rows, w_down, saved, x_rows, own, after):
    share, width = own[0].shape
    tile = 2 * TILE
    rows = sum(piece.shape[0] for piece in x_rows)
    half = pltpu.VMEM((share, rows), jnp.float32)
    return pl.pallas_call(
        whole_gradient_kernel,
        grid=(width // tile,),
        in_specs=[IN_SMEM]
        + [IN_HBM] * 12
        + [pl.BlockSpec((share, tile), lambda i: (0, i))] * 3
        + [IN_HBM],
        out_specs=[pl.BlockSpec((1, share, tile), lambda i: (0, 0, i))] * 3,
        out_shape=[jax.ShapeDtypeStruct((1, share, width), jnp.bfloat16)] * 3,
        scratch_shapes=[
            pltpu.VMEM((rows, width), jnp.bfloat16),
            pltpu.VMEM((rows, cot_rows[0].shape[1]), jnp.bfloat16),
            pltpu.VMEM((width, share), jnp.bfloat16),
            half,
            half,
            half,
            pltpu.VMEM((3, share, rows), jnp.bfloat16),
            pltpu.SemaphoreType.DMA((12,)),
        ],
        **kernel_params(
            8 * rows * share * width, 4 * rows * width + 12 * share * width, rows * share, 32
        ),
    )(
        place,
        *[left_out(value) for value in (*cot_rows, w_down)],
        *saved,
        *[left_out(value) for value in x_rows],
        *own,
        after,
    )


def dense_body(tokens, expert_ids, gate_weights, cotangent, w_gate, w_up, w_down):
    model_width = tokens.shape[1]
    experts = lax.axis_size("expert")
    groups = lax.axis_size("dp")
    share = w_gate.shape[1] // groups
    place = jnp.stack([lax.axis_index("expert"), lax.axis_index("dp")]).astype(jnp.int32)
    group, core, near, low, high = 1, 2, 4, 8, 16
    lanes = -(-experts // 128) * 128
    named = expert_ids[:, :, None] == jnp.arange(lanes, dtype=jnp.int32)[None, None, :]
    gate_table = jnp.sum(
        jnp.where(named, gate_weights.astype(jnp.float32)[:, :, None], 0.0), axis=1
    ).astype(jnp.bfloat16)

    def column_of(value):
        return [swap(value, high), swap(value, low | high), swap(value, low)]

    weights = (w_gate, w_up, w_down)
    packed = jnp.concatenate([cotangent, gate_table], axis=1)
    cot_mine_away = swap(packed, group)
    packed, cot_mine_away, *x_far = tied(packed, cot_mine_away, *column_of(tokens))
    x_column = jnp.concatenate([tokens, *x_far], axis=0)
    x_near = swap(x_column, near)
    x_column_away = swap(x_column, group)
    *cot_far, x_near, x_column_away = tied(*column_of(packed), x_near, x_column_away)
    x_near_away = swap(x_near, group)
    cot_column = jnp.concatenate([packed, *cot_far], axis=0)
    cot_far_away = column_of(cot_mine_away)
    cot_near = swap(cot_column, near)
    *kept_weights, x_rows, slope, swish, hidden = forward(
        [x_column, swap(x_column, core), x_near, swap(x_near, core)], weights
    )
    saved = (slope, swish, hidden)
    own_part, other_part, column_cot, column_lefts, token = backward(
        place, cot_column, swap(cot_column, core), saved, 0, kept_weights, place
    )
    column_own, column_given = own_part, swap(other_part, core)
    x_column_other = swap(x_column_away, core)
    cot_near, token, x_near_away, x_column_other = tied(
        cot_near, token, x_near_away, x_column_other
    )
    x_near_other = swap(x_near_away, core)
    cot_near_away = swap(cot_near, group)
    own_part, other_part, near_cot, near_lefts, _ = backward(
        place, cot_near, swap(cot_near, core), saved, 1, kept_weights, token
    )
    other_part, x_near_other, column_given = tied(other_part, x_near_other, column_given)
    near_partial = added(own_part, swap(other_part, core))
    partial = added(column_own, column_given, swap(near_partial, near))
    *own, token = own_gradients(
        place, [column_lefts, near_lefts], x_rows, [column_cot, near_cot], share
    )
    x_away = [x_column_away, x_near_away, x_column_other, x_near_other]
    *away_saved, token = away_forward(place, x_away, weights[:2], share, token)
    partial, token, cot_near_away, *cot_far_away = tied(
        partial, token, cot_near_away, *cot_far_away
    )
    cot_away = [jnp.concatenate([cot_mine_away, *cot_far_away], axis=0), cot_near_away]
    cot_away += [swap(value, core) for value in cot_away]
    grads = list(whole_gradients(place, cot_away, w_down, away_saved, x_away, own, token))
    block = partial.shape[0] // 4
    parts = [
        partial[:block],
        swap(partial[block : 2 * block], high),
        swap(partial[2 * block : 3 * block], low | high),
        swap(partial[3 * block :], low),
    ]
    *parts, grads[0] = tied(*parts, grads[0])
    result = added(*parts)
    token_grad = result[:, :model_width]
    gate_grad = jnp.sum(
        jnp.where(named, result[:, model_width:].astype(jnp.float32)[:, None, :], 0.0), axis=2
    ).astype(jnp.bfloat16)
    return (token_grad, gate_grad, *grads)


def body(tokens, expert_ids, *rest):
    tok_rows, top_count = expert_ids.shape
    if 2 * tok_rows * top_count // lax.axis_size("expert") < tok_rows:
        return routed_body(tokens, expert_ids, *rest)
    return dense_body(tokens, expert_ids, *rest)


def solution(mesh):
    return jax.shard_map(
        body,
        mesh=mesh,
        in_specs=(
            P(("expert", "dp"), None),
            P(("expert", "dp"), None),
            P(("expert", "dp"), None),
            P(("expert", "dp"), None),
            P("expert", None, None),
            P("expert", None, None),
            P("expert", None, None),
        ),
        out_specs=(
            P(("expert", "dp"), None),
            P(("expert", "dp"), None),
            P("expert", "dp", None),
            P("expert", "dp", None),
            P("expert", "dp", None),
        ),
        check_vma=False,
    )
```

```python
import functools

import jax
import jax.numpy as jnp
from jax import lax
from jax.experimental import pallas as pl
from jax.experimental.pallas import tpu as pltpu
from jax.sharding import PartitionSpec as P

TILE = 256
BOTH = ("expert", "dp")


def contract_last(left, right):
    return lax.dot_general(
        left, right, (((1,), (1,)), ((), ())), preferred_element_type=jnp.float32
    )


def contract_first(left, right):
    return lax.dot_general(
        left, right, (((0,), (0,)), ((), ())), preferred_element_type=jnp.float32
    )


def rounded(value):
    return lax.optimization_barrier(value.astype(jnp.bfloat16)).astype(jnp.float32)


def expert_forward(expert_rows, gate_mat, up_mat, down_mat):
    pre_gate = contract_last(expert_rows, gate_mat)
    pre_up = contract_last(expert_rows, up_mat)
    gate_sigmoid = jax.nn.sigmoid(pre_gate)
    hidden = (pre_gate * gate_sigmoid * pre_up).astype(jnp.bfloat16)
    outputs = contract_last(hidden, down_mat).astype(jnp.bfloat16)
    return (pre_gate, pre_up, gate_sigmoid, hidden, outputs)


def routed_body(tokens, expert_ids, gate_weights, cotangent, w_gate, w_up, w_down):
    tok_rows, top_count = expert_ids.shape
    model_width = tokens.shape[1]
    experts = lax.axis_size("expert")
    capacity = min(tok_rows, 2 * tok_rows * top_count // experts)
    slot_count = tok_rows * top_count
    buffer_rows = experts * capacity
    flat_ids = expert_ids.reshape(slot_count)
    onehot = (flat_ids[:, None] == jnp.arange(experts, dtype=jnp.int32)[None, :]).astype(jnp.int32)
    slot_rank = jnp.sum((jnp.cumsum(onehot, axis=0) - 1) * onehot, axis=1)
    position = flat_ids * capacity + slot_rank
    placing = (jnp.arange(buffer_rows, dtype=jnp.int32)[:, None] == position[None, :]).astype(
        jnp.bfloat16
    )
    token_map = placing.reshape(buffer_rows, tok_rows, top_count).sum(axis=2)
    x_send = jnp.dot(token_map, tokens, preferred_element_type=jnp.float32).astype(jnp.bfloat16)
    x_send = x_send.reshape(experts, capacity, model_width)
    cot_send = jnp.dot(token_map, cotangent, preferred_element_type=jnp.float32).astype(
        jnp.bfloat16
    )
    cot_send = cot_send.reshape(experts, capacity, model_width)
    gate_send = jnp.dot(
        placing, gate_weights.reshape(slot_count), preferred_element_type=jnp.float32
    )
    gate_send = gate_send.astype(jnp.bfloat16).reshape(experts, capacity)
    gate_mat = w_gate[0]
    up_mat = w_up[0]
    down_mat = w_down[0]
    x_recv = lax.all_to_all(x_send, "expert", split_axis=0, concat_axis=0, tiled=True)
    expert_rows = x_recv.reshape(buffer_rows, model_width)
    pre_gate, pre_up, gate_sigmoid, hidden, outputs = expert_forward(
        expert_rows, gate_mat, up_mat, down_mat
    )
    cot_recv, gate_recv = (
        lax.all_to_all(cot_send, "expert", split_axis=0, concat_axis=0, tiled=True),
        lax.all_to_all(gate_send, "expert", split_axis=0, concat_axis=0, tiled=True),
    )
    cot_rows = cot_recv.reshape(buffer_rows, model_width)
    gate_rows = gate_recv.reshape(buffer_rows).astype(jnp.float32)
    scaled = (gate_rows[:, None] * cot_rows.astype(jnp.float32)).astype(jnp.bfloat16)
    d_hidden = jnp.dot(scaled, down_mat, preferred_element_type=jnp.float32)
    d_pre_gate = (
        d_hidden * pre_up * gate_sigmoid * (1.0 + pre_gate * (1.0 - gate_sigmoid))
    ).astype(jnp.bfloat16)
    d_pre_up = (d_hidden * pre_gate * gate_sigmoid).astype(jnp.bfloat16)
    slot_grad = (
        jnp.dot(d_pre_gate, gate_mat, preferred_element_type=jnp.float32)
        + jnp.dot(d_pre_up, up_mat, preferred_element_type=jnp.float32)
    ).astype(jnp.bfloat16)
    pieces = []
    for operand, partner in ((d_pre_gate, expert_rows), (d_pre_up, expert_rows), (hidden, scaled)):
        pieces.append(rounded(contract_first(operand, partner)))
    summed = lax.psum_scatter(
        jnp.concatenate(pieces, axis=1).astype(jnp.bfloat16), "dp", scatter_dimension=0, tiled=True
    ).astype(jnp.float32)
    grad_gate = summed[:, :model_width].astype(jnp.bfloat16)[None]
    grad_up = summed[:, model_width : 2 * model_width].astype(jnp.bfloat16)[None]
    grad_down_t = summed[:, 2 * model_width :].astype(jnp.bfloat16)[None]
    slot_back = slot_grad.reshape(experts, capacity, model_width)
    out_send = outputs.reshape(experts, capacity, model_width)
    grad_back, out_back = (
        lax.all_to_all(slot_back, "expert", split_axis=0, concat_axis=0, tiled=True),
        lax.all_to_all(out_send, "expert", split_axis=0, concat_axis=0, tiled=True),
    )
    picked = out_back.reshape(buffer_rows, model_width)[position].astype(jnp.float32)
    picked = picked.reshape(tok_rows, top_count, model_width)
    gate_grad = jnp.sum(picked * cotangent.astype(jnp.float32)[:, None, :], axis=2).astype(
        jnp.bfloat16
    )
    gathered = grad_back.reshape(buffer_rows, model_width)[position].astype(jnp.float32)
    token_grad = gathered.reshape(tok_rows, top_count, model_width).sum(axis=1).astype(jnp.bfloat16)
    return (token_grad, gate_grad, grad_gate, grad_up, grad_down_t)


def swap(value, flip):
    count = lax.axis_size(BOTH)
    return lax.ppermute(value, BOTH, [(i, i ^ flip) for i in range(count)])


def added(*terms):
    return sum(term.astype(jnp.float32) for term in terms).astype(jnp.bfloat16)


def tied(*values):
    return lax.optimization_barrier(values)


def kernel_params(flops, moved, transcendentals=0, megabytes=14):
    return {
        "compiler_params": pltpu.CompilerParams(vmem_limit_bytes=megabytes * 1024 * 1024),
        "cost_estimate": pl.CostEstimate(
            flops=flops, bytes_accessed=moved, transcendentals=transcendentals
        ),
    }


IN_HBM = pl.BlockSpec(memory_space=pl.ANY)
IN_VMEM = pl.BlockSpec(memory_space=pltpu.VMEM)
IN_SMEM = pl.BlockSpec(memory_space=pltpu.SMEM)


def kept(value):
    return pltpu.with_memory_space_constraint(value, pltpu.VMEM)


def left_out(value):
    return pltpu.with_memory_space_constraint(value, pltpu.HBM)


def fetched(pairs, sems):
    copies = [pltpu.make_async_copy(src, dst, sems.at[i]) for i, (src, dst) in enumerate(pairs)]
    for copy in copies:
        copy.start()
    return copies


def placed(pieces, target):
    pairs, first = [], 0
    for piece in pieces:
        pairs.append((piece, target.at[pl.ds(first, piece.shape[0])]))
        first += piece.shape[0]
    return pairs


def as_cotangents(x_refs):
    views = []
    for column, near in (x_refs[:2], x_refs[2:]):
        block = column.shape[0] // 4
        views += [column.at[pl.ds(0, 2 * block)], near.at[pl.ds(0, block)]]
        views += [column.at[pl.ds(2 * block, 2 * block)], near.at[pl.ds(block, 3 * block)]]
    return views


def forward_kernel(*refs):
    pieces, weight_refs, weight_outs, sems = refs[:4], refs[4:7], refs[7:10], refs[-1]
    rows_out, slope_out, swish_out, hidden_out = refs[10:14]
    units = slope_out.shape[1]
    pairs = placed(pieces, rows_out)
    for start in range(0, units, TILE):
        for i in range(2):
            rows = pl.ds(start, TILE)
            pairs.append((weight_refs[i].at[0, rows], weight_outs[i].at[rows]))
    half = weight_outs[2].shape[0] // 2
    for i in range(2):
        rows = pl.ds(i * half, half)
        pairs.append((weight_refs[2].at[0, rows], weight_outs[2].at[rows]))
    copies = fetched(pairs, sems)
    for copy in copies[:4]:
        copy.wait()
    for step, start in enumerate(range(0, units, TILE)):
        for copy in copies[4 + 2 * step : 6 + 2 * step]:
            copy.wait()
        rows = rows_out[...]
        chunk = slice(start, start + TILE)
        pre_gate = contract_last(rows, weight_outs[0][chunk])
        pre_up = contract_last(rows, weight_outs[1][chunk])
        gate_sigmoid = jax.nn.sigmoid(pre_gate)
        swish = pre_gate * gate_sigmoid
        slope_out[:, chunk] = pre_up * gate_sigmoid * (1.0 + pre_gate * (1.0 - gate_sigmoid))
        swish_out[:, chunk] = swish
        hidden_out[:, chunk] = swish * pre_up
    for copy in copies[-2:]:
        copy.wait()


def forward(pieces, weights):
    _, units, width = weights[0].shape
    rows = sum(piece.shape[0] for piece in pieces)
    outs = [pltpu.VMEM((rows, units), jnp.float32)] * 3
    for shape in ((rows, width), (width, units), (units, width), (units, width)):
        outs.insert(0, pltpu.VMEM(shape, jnp.bfloat16))
    return pl.pallas_call(
        forward_kernel,
        in_specs=[IN_HBM] * 7,
        out_specs=[IN_VMEM] * 7,
        out_shape=outs,
        scratch_shapes=[pltpu.SemaphoreType.DMA((6 + 2 * (units // TILE),))],
        **kernel_params(4 * rows * units * width, 2 * rows * width, rows * units),
    )(*[left_out(value) for value in (*pieces, *weights)])


def backward_kernel(
    which,
    place_ref,
    own_ref,
    other_ref,
    slope_ref,
    swish_ref,
    hidden_ref,
    gate_ref,
    up_ref,
    down_ref,
    _,
    own_out,
    other_out,
    rows_out,
    lefts_out,
    token_out,
    sems,
):
    width, units = down_ref.shape
    half = own_ref.shape[0]
    lanes = own_ref.shape[1] - width
    copies = fetched(placed((own_ref, other_ref), rows_out), sems)
    token_out[...] = jnp.zeros_like(token_out)
    for copy in copies:
        copy.wait()
    saved = pl.ds(which * 2 * half, 2 * half)
    column = lax.broadcasted_iota(jnp.int32, (2 * half, lanes), 1) == place_ref[0]
    table = rows_out[:, width:].astype(jnp.float32)
    gates = jnp.sum(jnp.where(column, table, 0.0), axis=1, keepdims=True)
    score = jnp.zeros((2 * half, 1), jnp.float32)
    for start in range(0, units, TILE):
        chunk = slice(start, start + TILE)
        raw = jnp.dot(
            rows_out[:, :width], down_ref[:, chunk], preferred_element_type=jnp.float32
        )
        hidden = hidden_ref[saved, chunk]
        score += jnp.sum(hidden * raw, axis=1, keepdims=True)
        d_hidden = gates * raw
        lefts_out[:, chunk] = (d_hidden * slope_ref[saved, chunk]).astype(jnp.bfloat16)
        lefts_out[:, units + start : units + start + TILE] = (
            d_hidden * swish_ref[saved, chunk]
        ).astype(jnp.bfloat16)
        lefts_out[:, 2 * units + start : 2 * units + start + TILE] = (gates * hidden).astype(
            jnp.bfloat16
        )
    scores = jnp.where(column, score, 0.0).astype(jnp.bfloat16)
    own_out[:, width:] = scores[:half]
    other_out[:, width:] = scores[half:]
    for start in range(0, width, 2 * TILE):
        chunk = slice(start, start + 2 * TILE)
        total = (
            jnp.dot(lefts_out[:, :units], gate_ref[:, chunk], preferred_element_type=jnp.float32)
            + jnp.dot(
                lefts_out[:, units : 2 * units],
                up_ref[:, chunk],
                preferred_element_type=jnp.float32,
            )
        ).astype(jnp.bfloat16)
        own_out[:, chunk] = total[:half]
        other_out[:, chunk] = total[half:]


def backward(place, own, other, saved, which, weights, after):
    units, width = weights[0].shape
    half, packed = own.shape
    rows = 2 * half
    return pl.pallas_call(
        functools.partial(backward_kernel, which),
        in_specs=[IN_SMEM] + [IN_HBM] * 2 + [IN_VMEM] * 6 + [IN_HBM],
        out_specs=[IN_VMEM] * 5,
        out_shape=[
            jax.ShapeDtypeStruct((half, packed), jnp.bfloat16),
            jax.ShapeDtypeStruct((half, packed), jnp.bfloat16),
            pltpu.VMEM((rows, packed), jnp.bfloat16),
            pltpu.VMEM((rows, 3 * units), jnp.bfloat16),
            jax.ShapeDtypeStruct((8, 128), jnp.float32),
        ],
        scratch_shapes=[pltpu.SemaphoreType.DMA((2,))],
        **kernel_params(0, 0),
    )(place, own, other, *[kept(value) for value in (*saved, *weights)], after)


def own_gradient_kernel(place_ref, *refs):
    column_ref, near_ref, x_ref, column_cot, near_cot = refs[:5]
    x_refs, weight_refs = refs[5:9], refs[9:11]
    outs, (slope_out, swish_out, hidden_out, token_out) = refs[11:14], refs[14:18]
    lefts, rows, gate_ref, up_ref, sems = refs[18:]
    share, tile = outs[0].shape
    units = column_ref.shape[1] // 3
    start = pl.multiple_of(place_ref[1] * share, 128)
    own = pl.ds(start, share)
    copies = [
        pltpu.make_async_copy(source, target, sems.at[i])
        for i, (source, target) in enumerate(
            placed(as_cotangents(x_refs), rows)
            + [(weight_refs[0].at[0, own], gate_ref), (weight_refs[1].at[0, own], up_ref)]
        )
    ]

    @pl.when(pl.program_id(0) == 0)
    def _():
        for copy in copies:
            copy.start()
        token_out[...] = jnp.zeros_like(token_out)
        for i in range(3):
            lefts[i] = jnp.concatenate(
                [ref[:, pl.ds(start + i * units, share)] for ref in (column_ref, near_ref)], axis=0
            ).T

    chunk = pl.ds(pl.multiple_of(pl.program_id(0) * tile, tile), tile)
    cot_rows = jnp.concatenate([column_cot[:, chunk], near_cot[:, chunk]], axis=0)
    for i, right in enumerate((x_ref[:, chunk], x_ref[:, chunk], cot_rows)):
        outs[i][...] = jnp.dot(lefts[i], right, preferred_element_type=jnp.float32).astype(
            jnp.bfloat16
        )

    @pl.when(pl.program_id(0) == pl.num_programs(0) - 1)
    def _():
        for copy in copies:
            copy.wait()
        pre_gate = contract_last(gate_ref[...], rows[...])
        pre_up = contract_last(up_ref[...], rows[...])
        gate_sigmoid = jax.nn.sigmoid(pre_gate)
        swish = pre_gate * gate_sigmoid
        slope_out[...] = (pre_up * gate_sigmoid * (1.0 + pre_gate * (1.0 - gate_sigmoid))).astype(
            jnp.bfloat16
        )
        swish_out[...] = swish.astype(jnp.bfloat16)
        hidden_out[...] = (swish * pre_up).astype(jnp.bfloat16)


def own_gradients(place, lefts, x_rows, cot_rows, x_away, weights, share):
    rows, width = x_rows.shape
    tile = 2 * TILE
    half = pltpu.VMEM((share, width), jnp.bfloat16)
    return pl.pallas_call(
        own_gradient_kernel,
        grid=(width // tile,),
        in_specs=[IN_SMEM] + [IN_VMEM] * 5 + [IN_HBM] * 6,
        out_specs=[pl.BlockSpec((share, tile), lambda i: (0, i))] * 3
        + [pl.BlockSpec((share, rows), lambda i: (0, 0))] * 3
        + [pl.BlockSpec((8, 128), lambda i: (0, 0))],
        out_shape=[jax.ShapeDtypeStruct((share, width), jnp.bfloat16)] * 3
        + [jax.ShapeDtypeStruct((share, rows), jnp.bfloat16)] * 3
        + [jax.ShapeDtypeStruct((8, 128), jnp.float32)],
        scratch_shapes=[
            pltpu.VMEM((3, share, rows), jnp.bfloat16),
            pltpu.VMEM((rows, width), jnp.bfloat16),
            half,
            half,
            pltpu.SemaphoreType.DMA((10,)),
        ],
        **kernel_params(0, 0, 0, 24),
    )(
        place,
        *[kept(value) for value in (*lefts, x_rows, *cot_rows)],
        *[left_out(value) for value in (*x_away, *weights)],
    )


def whole_gradient_kernel(place_ref, *refs):
    cot_refs, down_ref, saved_refs, x_refs = refs[:6], refs[6], refs[7:10], refs[10:14]
    own_refs, outs = refs[14:17], refs[18:21]
    rows, cot, down, slope, swish, hidden, lefts, sems = refs[21:]
    share, tile = outs[0].shape[1:]
    width = rows.shape[1]

    @pl.when(pl.program_id(0) == 0)
    def _():
        own = pl.ds(pl.multiple_of(place_ref[1] * share, 128), share)
        copies = fetched(
            placed(cot_refs, cot)
            + [(down_ref.at[0, :, own], down)]
            + list(zip(saved_refs, (slope, swish, hidden)))
            + placed(as_cotangents(x_refs), rows),
            sems,
        )
        for copy in copies[:7]:
            copy.wait()
        table = cot[:, width:]
        pick = (lax.broadcasted_iota(jnp.int32, (16, table.shape[1]), 1) == place_ref[0]).astype(
            jnp.bfloat16
        )
        gates = contract_last(pick, table)[:1]
        raw = jnp.dot(cot[:, :width], down[...], preferred_element_type=jnp.float32).T
        d_hidden = gates * raw
        for copy in copies[7:10]:
            copy.wait()
        for i, factor in enumerate((slope, swish)):
            lefts[i] = (d_hidden * factor[...].astype(jnp.float32)).astype(jnp.bfloat16)
        lefts[2] = (gates * hidden[...].astype(jnp.float32)).astype(jnp.bfloat16)
        for copy in copies[10:]:
            copy.wait()

    first = pl.multiple_of(pl.program_id(0) * tile, tile)
    for i in range(3):
        right = rows if i < 2 else cot
        away = jnp.dot(lefts[i], right[:, pl.ds(first, tile)], preferred_element_type=jnp.float32)
        outs[i][0] = (own_refs[i][...].astype(jnp.float32) + away).astype(jnp.bfloat16)


def whole_gradients(place, cot_rows, w_down, saved, x_rows, own, after):
    share, width = own[0].shape
    tile = 2 * TILE
    rows = sum(piece.shape[0] for piece in x_rows)
    half = pltpu.VMEM((share, rows), jnp.bfloat16)
    return pl.pallas_call(
        whole_gradient_kernel,
        grid=(width // tile,),
        in_specs=[IN_SMEM]
        + [IN_HBM] * 14
        + [pl.BlockSpec((share, tile), lambda i: (0, i))] * 3
        + [IN_HBM],
        out_specs=[pl.BlockSpec((1, share, tile), lambda i: (0, 0, i))] * 3,
        out_shape=[jax.ShapeDtypeStruct((1, share, width), jnp.bfloat16)] * 3,
        scratch_shapes=[
            pltpu.VMEM((rows, width), jnp.bfloat16),
            pltpu.VMEM((rows, cot_rows[0].shape[1]), jnp.bfloat16),
            pltpu.VMEM((width, share), jnp.bfloat16),
            half,
            half,
            half,
            pltpu.VMEM((3, share, rows), jnp.bfloat16),
            pltpu.SemaphoreType.DMA((18,)),
        ],
        **kernel_params(
            8 * rows * share * width, 4 * rows * width + 12 * share * width, rows * share, 32
        ),
    )(
        place,
        *[left_out(value) for value in (*cot_rows, w_down)],
        *saved,
        *[left_out(value) for value in x_rows],
        *own,
        after,
    )


def dense_body(tokens, expert_ids, gate_weights, cotangent, w_gate, w_up, w_down):
    model_width = tokens.shape[1]
    experts = lax.axis_size("expert")
    groups = lax.axis_size("dp")
    share = w_gate.shape[1] // groups
    place = jnp.stack([lax.axis_index("expert"), lax.axis_index("dp")]).astype(jnp.int32)
    group, core, near, low, high = 1, 2, 4, 8, 16
    lanes = -(-experts // 128) * 128
    named = expert_ids.T[:, :, None] == jnp.arange(lanes, dtype=jnp.int32)[None, None, :]
    gate_table = jnp.sum(
        jnp.where(named, gate_weights.T.astype(jnp.float32)[:, :, None], 0.0), axis=0
    ).astype(jnp.bfloat16)

    def column_of(value):
        return [swap(value, high), swap(value, low), swap(value, low | high)]

    weights = (w_gate, w_up, w_down)
    packed = jnp.concatenate([cotangent, gate_table], axis=1)
    cot_mine_away = swap(packed, group)
    packed, cot_mine_away, *x_far = tied(packed, cot_mine_away, *column_of(tokens))
    x_column = jnp.concatenate([tokens, *x_far], axis=0)
    x_near = swap(x_column, near)
    x_column_away = swap(x_column, group)
    *cot_far, x_near, x_column_away = tied(*column_of(packed), x_near, x_column_away)
    x_near_away = swap(x_near, group)
    cot_column = jnp.concatenate([packed, *cot_far], axis=0)
    cot_high_away = swap(cot_mine_away, high)
    cot_near = swap(cot_column, near)
    *kept_weights, x_rows, slope, swish, hidden = forward(
        [x_column, swap(x_column, core), x_near, swap(x_near, core)], weights
    )
    saved = (slope, swish, hidden)
    own_part, other_part, column_cot, column_lefts, token = backward(
        place, cot_column, swap(cot_column, core), saved, 0, kept_weights, place
    )
    column_own, column_given = own_part, swap(other_part, core)
    x_column_other = swap(x_column_away, core)
    cot_near, token, x_near_away, x_column_other, cot_high_away = tied(
        cot_near, token, x_near_away, x_column_other, cot_high_away
    )
    cot_first_away = jnp.concatenate([cot_mine_away, cot_high_away], axis=0)
    cot_second_away, cot_first_other = swap(cot_first_away, low), swap(cot_first_away, core)
    x_near_other = swap(x_near_away, core)
    near_mine_away = swap(cot_mine_away, near)
    near_far_away = swap(cot_near[packed.shape[0] :], group)
    own_part, other_part, near_cot, near_lefts, _ = backward(
        place, cot_near, swap(cot_near, core), saved, 1, kept_weights, token
    )
    other_part, x_near_other, column_given, cot_first_other, near_mine_away = tied(
        other_part, x_near_other, column_given, cot_first_other, near_mine_away
    )
    near_mine_other = swap(near_mine_away, core)
    near_sum = added(own_part, swap(other_part, core))
    partial = added(column_own, column_given, swap(near_sum, near))
    block = packed.shape[0]
    x_away = [x_column_away, x_near_away, x_column_other, x_near_other]
    *own, slope, swish, hidden, token = own_gradients(
        place,
        [column_lefts, near_lefts],
        x_rows,
        [column_cot, near_cot],
        x_away,
        weights[:2],
        share,
    )
    cot_second_away, near_far_away, near_mine_other, partial, token = tied(
        cot_second_away, near_far_away, near_mine_other, partial, token
    )
    cot_rest_away = jnp.concatenate([cot_second_away, near_far_away], axis=0)
    cot_away = [cot_first_away, near_mine_away, cot_rest_away]
    cot_away += [cot_first_other, near_mine_other, swap(cot_rest_away, core)]
    saved = (slope, swish, hidden)
    grads = list(whole_gradients(place, cot_away, w_down, saved, x_away, own, token))
    parts = [
        partial[:block],
        swap(partial[block : 2 * block], high),
        swap(partial[2 * block : 3 * block], low),
        swap(partial[3 * block :], low | high),
    ]
    *parts, grads[0] = tied(*parts, grads[0])
    token_grad = added(*[value[:, :model_width] for value in parts])
    scores = added(*[value[:, model_width:] for value in parts]).astype(jnp.float32)
    gate_grad = jnp.sum(jnp.where(named, scores[None], 0.0), axis=2).astype(jnp.bfloat16)
    return (token_grad, gate_grad.T, *grads)


def body(tokens, expert_ids, *rest):
    tok_rows, top_count = expert_ids.shape
    if 2 * tok_rows * top_count // lax.axis_size("expert") < tok_rows:
        return routed_body(tokens, expert_ids, *rest)
    return dense_body(tokens, expert_ids, *rest)


def solution(mesh):
    return jax.shard_map(
        body,
        mesh=mesh,
        in_specs=(
            P(("expert", "dp"), None),
            P(("expert", "dp"), None),
            P(("expert", "dp"), None),
            P(("expert", "dp"), None),
            P("expert", None, None),
            P("expert", None, None),
            P("expert", None, None),
        ),
        out_specs=(
            P(("expert", "dp"), None),
            P(("expert", "dp"), None),
            P("expert", "dp", None),
            P("expert", "dp", None),
            P("expert", "dp", None),
        ),
        check_vma=False,
    )
```

```python
import functools

import jax
import jax.numpy as jnp
from jax import lax
from jax.experimental import pallas as pl
from jax.experimental.pallas import tpu as pltpu
from jax.sharding import PartitionSpec as P

TILE = 256
BOTH = ("expert", "dp")


def contract_last(left, right):
    return lax.dot_general(
        left, right, (((1,), (1,)), ((), ())), preferred_element_type=jnp.float32
    )


def contract_first(left, right):
    return lax.dot_general(
        left, right, (((0,), (0,)), ((), ())), preferred_element_type=jnp.float32
    )


def rounded(value):
    return lax.optimization_barrier(value.astype(jnp.bfloat16)).astype(jnp.float32)


def expert_forward(expert_rows, gate_mat, up_mat, down_mat):
    pre_gate = contract_last(expert_rows, gate_mat)
    pre_up = contract_last(expert_rows, up_mat)
    gate_sigmoid = jax.nn.sigmoid(pre_gate)
    hidden = (pre_gate * gate_sigmoid * pre_up).astype(jnp.bfloat16)
    outputs = contract_last(hidden, down_mat).astype(jnp.bfloat16)
    return (pre_gate, pre_up, gate_sigmoid, hidden, outputs)


def routed_body(tokens, expert_ids, gate_weights, cotangent, w_gate, w_up, w_down):
    tok_rows, top_count = expert_ids.shape
    model_width = tokens.shape[1]
    experts = lax.axis_size("expert")
    capacity = min(tok_rows, 2 * tok_rows * top_count // experts)
    slot_count = tok_rows * top_count
    buffer_rows = experts * capacity
    flat_ids = expert_ids.reshape(slot_count)
    onehot = (flat_ids[:, None] == jnp.arange(experts, dtype=jnp.int32)[None, :]).astype(jnp.int32)
    slot_rank = jnp.sum((jnp.cumsum(onehot, axis=0) - 1) * onehot, axis=1)
    position = flat_ids * capacity + slot_rank
    placing = (jnp.arange(buffer_rows, dtype=jnp.int32)[:, None] == position[None, :]).astype(
        jnp.bfloat16
    )
    token_map = placing.reshape(buffer_rows, tok_rows, top_count).sum(axis=2)
    x_send = jnp.dot(token_map, tokens, preferred_element_type=jnp.float32).astype(jnp.bfloat16)
    x_send = x_send.reshape(experts, capacity, model_width)
    cot_send = jnp.dot(token_map, cotangent, preferred_element_type=jnp.float32).astype(
        jnp.bfloat16
    )
    cot_send = cot_send.reshape(experts, capacity, model_width)
    gate_send = jnp.dot(
        placing, gate_weights.reshape(slot_count), preferred_element_type=jnp.float32
    )
    gate_send = gate_send.astype(jnp.bfloat16).reshape(experts, capacity)
    gate_mat = w_gate[0]
    up_mat = w_up[0]
    down_mat = w_down[0]
    x_recv = lax.all_to_all(x_send, "expert", split_axis=0, concat_axis=0, tiled=True)
    expert_rows = x_recv.reshape(buffer_rows, model_width)
    pre_gate, pre_up, gate_sigmoid, hidden, outputs = expert_forward(
        expert_rows, gate_mat, up_mat, down_mat
    )
    cot_recv, gate_recv = (
        lax.all_to_all(cot_send, "expert", split_axis=0, concat_axis=0, tiled=True),
        lax.all_to_all(gate_send, "expert", split_axis=0, concat_axis=0, tiled=True),
    )
    cot_rows = cot_recv.reshape(buffer_rows, model_width)
    gate_rows = gate_recv.reshape(buffer_rows).astype(jnp.float32)
    scaled = (gate_rows[:, None] * cot_rows.astype(jnp.float32)).astype(jnp.bfloat16)
    d_hidden = jnp.dot(scaled, down_mat, preferred_element_type=jnp.float32)
    d_pre_gate = (
        d_hidden * pre_up * gate_sigmoid * (1.0 + pre_gate * (1.0 - gate_sigmoid))
    ).astype(jnp.bfloat16)
    d_pre_up = (d_hidden * pre_gate * gate_sigmoid).astype(jnp.bfloat16)
    slot_grad = (
        jnp.dot(d_pre_gate, gate_mat, preferred_element_type=jnp.float32)
        + jnp.dot(d_pre_up, up_mat, preferred_element_type=jnp.float32)
    ).astype(jnp.bfloat16)
    pieces = []
    for operand, partner in ((d_pre_gate, expert_rows), (d_pre_up, expert_rows), (hidden, scaled)):
        pieces.append(rounded(contract_first(operand, partner)))
    summed = lax.psum_scatter(
        jnp.concatenate(pieces, axis=1).astype(jnp.bfloat16), "dp", scatter_dimension=0, tiled=True
    ).astype(jnp.float32)
    grad_gate = summed[:, :model_width].astype(jnp.bfloat16)[None]
    grad_up = summed[:, model_width : 2 * model_width].astype(jnp.bfloat16)[None]
    grad_down_t = summed[:, 2 * model_width :].astype(jnp.bfloat16)[None]
    slot_back = slot_grad.reshape(experts, capacity, model_width)
    out_send = outputs.reshape(experts, capacity, model_width)
    grad_back, out_back = (
        lax.all_to_all(slot_back, "expert", split_axis=0, concat_axis=0, tiled=True),
        lax.all_to_all(out_send, "expert", split_axis=0, concat_axis=0, tiled=True),
    )
    picked = out_back.reshape(buffer_rows, model_width)[position].astype(jnp.float32)
    picked = picked.reshape(tok_rows, top_count, model_width)
    gate_grad = jnp.sum(picked * cotangent.astype(jnp.float32)[:, None, :], axis=2).astype(
        jnp.bfloat16
    )
    gathered = grad_back.reshape(buffer_rows, model_width)[position].astype(jnp.float32)
    token_grad = gathered.reshape(tok_rows, top_count, model_width).sum(axis=1).astype(jnp.bfloat16)
    return (token_grad, gate_grad, grad_gate, grad_up, grad_down_t)


def swap(value, flip):
    count = lax.axis_size(BOTH)
    return lax.ppermute(value, BOTH, [(i, i ^ flip) for i in range(count)])


def added(*terms):
    return sum(term.astype(jnp.float32) for term in terms).astype(jnp.bfloat16)


def tied(*values):
    return lax.optimization_barrier(values)


def kernel_params(flops, moved, transcendentals=0, megabytes=14):
    return {
        "compiler_params": pltpu.CompilerParams(vmem_limit_bytes=megabytes * 1024 * 1024),
        "cost_estimate": pl.CostEstimate(
            flops=flops, bytes_accessed=moved, transcendentals=transcendentals
        ),
    }


IN_HBM = pl.BlockSpec(memory_space=pl.ANY)
IN_VMEM = pl.BlockSpec(memory_space=pltpu.VMEM)
IN_SMEM = pl.BlockSpec(memory_space=pltpu.SMEM)


def kept(value):
    return pltpu.with_memory_space_constraint(value, pltpu.VMEM)


def left_out(value):
    return pltpu.with_memory_space_constraint(value, pltpu.HBM)


def fetched(pairs, sems):
    copies = [pltpu.make_async_copy(src, dst, sems.at[i]) for i, (src, dst) in enumerate(pairs)]
    for copy in copies:
        copy.start()
    return copies


def placed(pieces, target):
    pairs, first = [], 0
    for piece in pieces:
        pairs.append((piece, target.at[pl.ds(first, piece.shape[0])]))
        first += piece.shape[0]
    return pairs


def as_cotangents(x_refs):
    views = []
    for column, near in (x_refs[:2], x_refs[2:]):
        block = column.shape[0] // 4
        views += [column.at[pl.ds(0, 2 * block)], near.at[pl.ds(0, block)]]
        views += [column.at[pl.ds(2 * block, 2 * block)], near.at[pl.ds(block, 3 * block)]]
    return views


def forward_kernel(*refs):
    pieces, weight_refs, weight_outs, sems = refs[:4], refs[4:7], refs[7:10], refs[-1]
    rows_out, slope_out, swish_out, hidden_out = refs[10:14]
    units = slope_out.shape[1]
    pairs = placed(pieces, rows_out)
    for start in range(0, units, TILE):
        for i in range(2):
            rows = pl.ds(start, TILE)
            pairs.append((weight_refs[i].at[0, rows], weight_outs[i].at[rows]))
    half = weight_outs[2].shape[0] // 2
    for i in range(2):
        rows = pl.ds(i * half, half)
        pairs.append((weight_refs[2].at[0, rows], weight_outs[2].at[rows]))
    copies = fetched(pairs, sems)
    for copy in copies[:4]:
        copy.wait()
    for step, start in enumerate(range(0, units, TILE)):
        for copy in copies[4 + 2 * step : 6 + 2 * step]:
            copy.wait()
        rows = rows_out[...]
        chunk = slice(start, start + TILE)
        pre_gate = contract_last(rows, weight_outs[0][chunk])
        pre_up = contract_last(rows, weight_outs[1][chunk])
        gate_sigmoid = jax.nn.sigmoid(pre_gate)
        swish = pre_gate * gate_sigmoid
        slope_out[:, chunk] = pre_up * gate_sigmoid * (1.0 + pre_gate * (1.0 - gate_sigmoid))
        swish_out[:, chunk] = swish
        hidden_out[:, chunk] = swish * pre_up
    for copy in copies[-2:]:
        copy.wait()


def forward(pieces, weights):
    _, units, width = weights[0].shape
    rows = sum(piece.shape[0] for piece in pieces)
    outs = [pltpu.VMEM((rows, units), jnp.float32)] * 3
    for shape in ((rows, width), (width, units), (units, width), (units, width)):
        outs.insert(0, pltpu.VMEM(shape, jnp.bfloat16))
    return pl.pallas_call(
        forward_kernel,
        in_specs=[IN_HBM] * 7,
        out_specs=[IN_VMEM] * 7,
        out_shape=outs,
        scratch_shapes=[pltpu.SemaphoreType.DMA((6 + 2 * (units // TILE),))],
        **kernel_params(4 * rows * units * width, 2 * rows * width, rows * units),
    )(*[left_out(value) for value in (*pieces, *weights)])


def backward_kernel(first, count, place_ref, *refs):
    pieces, (slope_ref, swish_ref, hidden_ref) = refs[:count], refs[count : count + 3]
    gate_ref, up_ref, down_ref, _ = refs[count + 3 : count + 7]
    parts_out, (rows_out, lefts_out, token_out, sems) = refs[count + 7 : -4], refs[-4:]
    width, units = down_ref.shape
    rows, packed = rows_out.shape
    copies = fetched(placed(pieces, rows_out), sems)
    token_out[...] = jnp.zeros_like(token_out)
    for copy in copies:
        copy.wait()
    saved = slice(first, first + rows)
    column = lax.broadcasted_iota(jnp.int32, (rows, packed - width), 1) == place_ref[0]
    table = rows_out[:, width:].astype(jnp.float32)
    gates = jnp.sum(jnp.where(column, table, 0.0), axis=1, keepdims=True)
    score = jnp.zeros((rows, 1), jnp.float32)
    for start in range(0, units, TILE):
        chunk = slice(start, start + TILE)
        raw = jnp.dot(
            rows_out[:, :width], down_ref[:, chunk], preferred_element_type=jnp.float32
        )
        hidden = hidden_ref[saved, chunk]
        score += jnp.sum(hidden * raw, axis=1, keepdims=True)
        d_hidden = gates * raw
        lefts_out[:, chunk] = (d_hidden * slope_ref[saved, chunk]).astype(jnp.bfloat16)
        lefts_out[:, units + start : units + start + TILE] = (
            d_hidden * swish_ref[saved, chunk]
        ).astype(jnp.bfloat16)
        lefts_out[:, 2 * units + start : 2 * units + start + TILE] = (gates * hidden).astype(
            jnp.bfloat16
        )
    scores = jnp.where(column, score, 0.0).astype(jnp.bfloat16)
    block = rows // count
    for i, part in enumerate(parts_out):
        part[:, width:] = scores[i * block : (i + 1) * block]
    for start in range(0, width, 2 * TILE):
        chunk = slice(start, start + 2 * TILE)
        total = (
            jnp.dot(lefts_out[:, :units], gate_ref[:, chunk], preferred_element_type=jnp.float32)
            + jnp.dot(
                lefts_out[:, units : 2 * units],
                up_ref[:, chunk],
                preferred_element_type=jnp.float32,
            )
        ).astype(jnp.bfloat16)
        for i, part in enumerate(parts_out):
            part[:, chunk] = total[i * block : (i + 1) * block]


def backward(place, pieces, saved, first, weights, after):
    units, width = weights[0].shape
    count = len(pieces)
    block, packed = pieces[0].shape
    rows = count * block
    return pl.pallas_call(
        functools.partial(backward_kernel, first, count),
        in_specs=[IN_SMEM] + [IN_HBM] * count + [IN_VMEM] * 6 + [IN_HBM],
        out_specs=[IN_VMEM] * (count + 3),
        out_shape=[jax.ShapeDtypeStruct((block, packed), jnp.bfloat16)] * count
        + [
            pltpu.VMEM((rows, packed), jnp.bfloat16),
            pltpu.VMEM((rows, 3 * units), jnp.bfloat16),
            jax.ShapeDtypeStruct((8, 128), jnp.float32),
        ],
        scratch_shapes=[pltpu.SemaphoreType.DMA((count,))],
        **kernel_params(0, 0),
    )(place, *pieces, *[kept(value) for value in (*saved, *weights)], after)


def own_gradient_kernel(place_ref, *refs):
    left_refs, x_ref, own_cot_refs = refs[:3], refs[3], refs[4:7]
    x_refs, weight_refs = refs[7:11], refs[11:13]
    outs, (slope_out, swish_out, hidden_out, token_out) = refs[13:16], refs[16:20]
    lefts, rows, gate_ref, up_ref, sems = refs[20:]
    share, tile = outs[0].shape
    units = left_refs[0].shape[1] // 3
    start = pl.multiple_of(place_ref[1] * share, 128)
    own = pl.ds(start, share)
    copies = [
        pltpu.make_async_copy(source, target, sems.at[i])
        for i, (source, target) in enumerate(
            placed(as_cotangents(x_refs), rows)
            + [(weight_refs[0].at[0, own], gate_ref), (weight_refs[1].at[0, own], up_ref)]
        )
    ]

    @pl.when(pl.program_id(0) == 0)
    def _():
        for copy in copies:
            copy.start()
        token_out[...] = jnp.zeros_like(token_out)
        for i in range(3):
            lefts[i] = jnp.concatenate(
                [ref[:, pl.ds(start + i * units, share)] for ref in left_refs], axis=0
            ).T

    chunk = pl.ds(pl.multiple_of(pl.program_id(0) * tile, tile), tile)
    cot_rows = jnp.concatenate([ref[:, chunk] for ref in own_cot_refs], axis=0)
    for i, right in enumerate((x_ref[:, chunk], x_ref[:, chunk], cot_rows)):
        outs[i][...] = jnp.dot(lefts[i], right, preferred_element_type=jnp.float32).astype(
            jnp.bfloat16
        )

    @pl.when(pl.program_id(0) == pl.num_programs(0) - 1)
    def _():
        for copy in copies:
            copy.wait()
        pre_gate = contract_last(gate_ref[...], rows[...])
        pre_up = contract_last(up_ref[...], rows[...])
        gate_sigmoid = jax.nn.sigmoid(pre_gate)
        swish = pre_gate * gate_sigmoid
        slope_out[...] = (pre_up * gate_sigmoid * (1.0 + pre_gate * (1.0 - gate_sigmoid))).astype(
            jnp.bfloat16
        )
        swish_out[...] = swish.astype(jnp.bfloat16)
        hidden_out[...] = (swish * pre_up).astype(jnp.bfloat16)


def own_gradients(place, lefts, x_rows, cot_rows, x_away, weights, share):
    rows, width = x_rows.shape
    tile = 2 * TILE
    half = pltpu.VMEM((share, width), jnp.bfloat16)
    return pl.pallas_call(
        own_gradient_kernel,
        grid=(width // tile,),
        in_specs=[IN_SMEM] + [IN_VMEM] * 7 + [IN_HBM] * 6,
        out_specs=[pl.BlockSpec((share, tile), lambda i: (0, i))] * 3
        + [pl.BlockSpec((share, rows), lambda i: (0, 0))] * 3
        + [pl.BlockSpec((8, 128), lambda i: (0, 0))],
        out_shape=[jax.ShapeDtypeStruct((share, width), jnp.bfloat16)] * 3
        + [jax.ShapeDtypeStruct((share, rows), jnp.bfloat16)] * 3
        + [jax.ShapeDtypeStruct((8, 128), jnp.float32)],
        scratch_shapes=[
            pltpu.VMEM((3, share, rows), jnp.bfloat16),
            pltpu.VMEM((rows, width), jnp.bfloat16),
            half,
            half,
            pltpu.SemaphoreType.DMA((10,)),
        ],
        **kernel_params(0, 0, 0, 24),
    )(
        place,
        *[kept(value) for value in (*lefts, x_rows, *cot_rows)],
        *[left_out(value) for value in (*x_away, *weights)],
    )


def whole_gradient_kernel(place_ref, *refs):
    cot_refs, down_ref, saved_refs, x_refs = refs[:6], refs[6], refs[7:10], refs[10:14]
    own_refs, outs = refs[14:17], refs[18:21]
    rows, cot, down, slope, swish, hidden, lefts, sems = refs[21:]
    share, tile = outs[0].shape[1:]
    width = rows.shape[1]

    @pl.when(pl.program_id(0) == 0)
    def _():
        own = pl.ds(pl.multiple_of(place_ref[1] * share, 128), share)
        copies = fetched(
            placed(cot_refs, cot)
            + [(down_ref.at[0, :, own], down)]
            + list(zip(saved_refs, (slope, swish, hidden)))
            + placed(as_cotangents(x_refs), rows),
            sems,
        )
        for copy in copies[:7]:
            copy.wait()
        table = cot[:, width:]
        pick = (lax.broadcasted_iota(jnp.int32, (16, table.shape[1]), 1) == place_ref[0]).astype(
            jnp.bfloat16
        )
        gates = contract_last(pick, table)[:1]
        raw = jnp.dot(cot[:, :width], down[...], preferred_element_type=jnp.float32).T
        d_hidden = gates * raw
        for copy in copies[7:10]:
            copy.wait()
        for i, factor in enumerate((slope, swish)):
            lefts[i] = (d_hidden * factor[...].astype(jnp.float32)).astype(jnp.bfloat16)
        lefts[2] = (gates * hidden[...].astype(jnp.float32)).astype(jnp.bfloat16)
        for copy in copies[10:]:
            copy.wait()

    first = pl.multiple_of(pl.program_id(0) * tile, tile)
    for i in range(3):
        right = rows if i < 2 else cot
        away = jnp.dot(lefts[i], right[:, pl.ds(first, tile)], preferred_element_type=jnp.float32)
        outs[i][0] = (own_refs[i][...].astype(jnp.float32) + away).astype(jnp.bfloat16)


def whole_gradients(place, cot_rows, w_down, saved, x_rows, own, after):
    share, width = own[0].shape
    tile = 2 * TILE
    rows = sum(piece.shape[0] for piece in x_rows)
    half = pltpu.VMEM((share, rows), jnp.bfloat16)
    return pl.pallas_call(
        whole_gradient_kernel,
        grid=(width // tile,),
        in_specs=[IN_SMEM]
        + [IN_HBM] * 14
        + [pl.BlockSpec((share, tile), lambda i: (0, i))] * 3
        + [IN_HBM],
        out_specs=[pl.BlockSpec((1, share, tile), lambda i: (0, 0, i))] * 3,
        out_shape=[jax.ShapeDtypeStruct((1, share, width), jnp.bfloat16)] * 3,
        scratch_shapes=[
            pltpu.VMEM((rows, width), jnp.bfloat16),
            pltpu.VMEM((rows, cot_rows[0].shape[1]), jnp.bfloat16),
            pltpu.VMEM((width, share), jnp.bfloat16),
            half,
            half,
            half,
            pltpu.VMEM((3, share, rows), jnp.bfloat16),
            pltpu.SemaphoreType.DMA((18,)),
        ],
        **kernel_params(
            8 * rows * share * width, 4 * rows * width + 12 * share * width, rows * share, 32
        ),
    )(
        place,
        *[left_out(value) for value in (*cot_rows, w_down)],
        *saved,
        *[left_out(value) for value in x_rows],
        *own,
        after,
    )


def dense_body(tokens, expert_ids, gate_weights, cotangent, w_gate, w_up, w_down):
    model_width = tokens.shape[1]
    experts = lax.axis_size("expert")
    groups = lax.axis_size("dp")
    share = w_gate.shape[1] // groups
    place = jnp.stack([lax.axis_index("expert"), lax.axis_index("dp")]).astype(jnp.int32)
    group, core, near, low, high = 1, 2, 4, 8, 16
    lanes = -(-experts // 128) * 128
    named = expert_ids.T[:, :, None] == jnp.arange(lanes, dtype=jnp.int32)[None, None, :]
    gate_table = jnp.sum(
        jnp.where(named, gate_weights.T.astype(jnp.float32)[:, :, None], 0.0), axis=0
    ).astype(jnp.bfloat16)

    def column_of(value):
        return [swap(value, high), swap(value, low), swap(value, low | high)]

    weights = (w_gate, w_up, w_down)
    packed = jnp.concatenate([cotangent, gate_table], axis=1)
    x_high, x_low, x_both = column_of(tokens)
    packed, x_low = tied(packed, x_low)
    cot_mine_away, near_mine_away = swap(packed, group), swap(packed, group | near)
    packed, cot_mine_away, near_mine_away, x_high, x_low, x_both = tied(
        packed, cot_mine_away, near_mine_away, x_high, x_low, x_both
    )
    x_column = jnp.concatenate([tokens, x_high, x_low, x_both], axis=0)
    x_near = swap(x_column, near)
    x_column_away = swap(x_column, group)
    *cot_far, x_near, x_column_away = tied(*column_of(packed), x_near, x_column_away)
    x_near_away = swap(x_near, group)
    cot_column = jnp.concatenate([packed, *cot_far], axis=0)
    cot_high_away = swap(cot_mine_away, high)
    cot_near = swap(cot_column, near)
    *kept_weights, x_rows, slope, swish, hidden = forward(
        [x_column, swap(x_column, core), x_near, swap(x_near, core)], weights
    )
    saved = (slope, swish, hidden)
    own_part, other_part, column_cot, column_lefts, token = backward(
        place, [cot_column, swap(cot_column, core)], saved, 0, kept_weights, place
    )
    column_own, column_given = own_part, swap(other_part, core)
    x_column_other = swap(x_column_away, core)
    cot_near, token, x_near_away, x_column_other, cot_high_away = tied(
        cot_near, token, x_near_away, x_column_other, cot_high_away
    )
    cot_first_away = jnp.concatenate([cot_mine_away, cot_high_away], axis=0)
    cot_second_away, cot_first_other = swap(cot_first_away, low), swap(cot_first_away, core)
    x_near_other = swap(x_near_away, core)
    near_mine_other = swap(near_mine_away, core)
    near_far_away = swap(cot_near[packed.shape[0] :], group)
    half = x_rows.shape[0] // 2
    other_part, other_cot, other_lefts, _ = backward(
        place, [swap(cot_near, core)], saved, half + half // 2, kept_weights, token
    )
    own_part, own_cot, own_lefts, _ = backward(
        place, [cot_near], saved, half, kept_weights, token
    )
    other_part, x_near_other, column_given, cot_first_other, near_mine_other = tied(
        other_part, x_near_other, column_given, cot_first_other, near_mine_other
    )
    near_sum = added(own_part, swap(other_part, core))
    partial = added(column_own, column_given, swap(near_sum, near))
    block = packed.shape[0]
    x_away = [x_column_away, x_near_away, x_column_other, x_near_other]
    *own, slope, swish, hidden, token = own_gradients(
        place,
        [column_lefts, own_lefts, other_lefts],
        x_rows,
        [column_cot, own_cot, other_cot],
        x_away,
        weights[:2],
        share,
    )
    cot_second_away, near_far_away, partial, token = tied(
        cot_second_away, near_far_away, partial, token
    )
    cot_rest_away = jnp.concatenate([cot_second_away, near_far_away], axis=0)
    cot_away = [cot_first_away, near_mine_away, cot_rest_away]
    cot_away += [cot_first_other, near_mine_other, swap(cot_rest_away, core)]
    saved = (slope, swish, hidden)
    grads = list(whole_gradients(place, cot_away, w_down, saved, x_away, own, token))
    parts = [
        partial[:block],
        swap(partial[block : 2 * block], high),
        swap(partial[2 * block : 3 * block], low),
        swap(partial[3 * block :], low | high),
    ]
    *parts, grads[0] = tied(*parts, grads[0])
    token_grad = added(*[value[:, :model_width] for value in parts])
    scores = added(*[value[:, model_width:] for value in parts]).astype(jnp.float32)
    gate_grad = jnp.sum(jnp.where(named, scores[None], 0.0), axis=2).astype(jnp.bfloat16)
    return (token_grad, gate_grad.T, *grads)


def body(tokens, expert_ids, *rest):
    tok_rows, top_count = expert_ids.shape
    if 2 * tok_rows * top_count // lax.axis_size("expert") < tok_rows:
        return routed_body(tokens, expert_ids, *rest)
    return dense_body(tokens, expert_ids, *rest)


def solution(mesh):
    return jax.shard_map(
        body,
        mesh=mesh,
        in_specs=(
            P(("expert", "dp"), None),
            P(("expert", "dp"), None),
            P(("expert", "dp"), None),
            P(("expert", "dp"), None),
            P("expert", None, None),
            P("expert", None, None),
            P("expert", None, None),
        ),
        out_specs=(
            P(("expert", "dp"), None),
            P(("expert", "dp"), None),
            P("expert", "dp", None),
            P("expert", "dp", None),
            P("expert", "dp", None),
        ),
        check_vma=False,
    )
```

```python
import functools

import jax
import jax.numpy as jnp
from jax import lax
from jax.experimental import pallas as pl
from jax.experimental.pallas import tpu as pltpu
from jax.sharding import PartitionSpec as P

TILE = 256
BOTH = ("expert", "dp")


def contract_last(left, right):
    return lax.dot_general(
        left, right, (((1,), (1,)), ((), ())), preferred_element_type=jnp.float32
    )


def contract_first(left, right):
    return lax.dot_general(
        left, right, (((0,), (0,)), ((), ())), preferred_element_type=jnp.float32
    )


def rounded(value):
    return lax.optimization_barrier(value.astype(jnp.bfloat16)).astype(jnp.float32)


def expert_forward(expert_rows, gate_mat, up_mat, down_mat):
    pre_gate = contract_last(expert_rows, gate_mat)
    pre_up = contract_last(expert_rows, up_mat)
    gate_sigmoid = jax.nn.sigmoid(pre_gate)
    hidden = (pre_gate * gate_sigmoid * pre_up).astype(jnp.bfloat16)
    outputs = contract_last(hidden, down_mat).astype(jnp.bfloat16)
    return (pre_gate, pre_up, gate_sigmoid, hidden, outputs)


def routed_body(tokens, expert_ids, gate_weights, cotangent, w_gate, w_up, w_down):
    tok_rows, top_count = expert_ids.shape
    model_width = tokens.shape[1]
    experts = lax.axis_size("expert")
    capacity = min(tok_rows, 2 * tok_rows * top_count // experts)
    slot_count = tok_rows * top_count
    buffer_rows = experts * capacity
    flat_ids = expert_ids.reshape(slot_count)
    onehot = (flat_ids[:, None] == jnp.arange(experts, dtype=jnp.int32)[None, :]).astype(jnp.int32)
    slot_rank = jnp.sum((jnp.cumsum(onehot, axis=0) - 1) * onehot, axis=1)
    position = flat_ids * capacity + slot_rank
    placing = (jnp.arange(buffer_rows, dtype=jnp.int32)[:, None] == position[None, :]).astype(
        jnp.bfloat16
    )
    token_map = placing.reshape(buffer_rows, tok_rows, top_count).sum(axis=2)
    x_send = jnp.dot(token_map, tokens, preferred_element_type=jnp.float32).astype(jnp.bfloat16)
    x_send = x_send.reshape(experts, capacity, model_width)
    cot_send = jnp.dot(token_map, cotangent, preferred_element_type=jnp.float32).astype(
        jnp.bfloat16
    )
    cot_send = cot_send.reshape(experts, capacity, model_width)
    gate_send = jnp.dot(
        placing, gate_weights.reshape(slot_count), preferred_element_type=jnp.float32
    )
    gate_send = gate_send.astype(jnp.bfloat16).reshape(experts, capacity)
    gate_mat = w_gate[0]
    up_mat = w_up[0]
    down_mat = w_down[0]
    x_recv = lax.all_to_all(x_send, "expert", split_axis=0, concat_axis=0, tiled=True)
    expert_rows = x_recv.reshape(buffer_rows, model_width)
    pre_gate, pre_up, gate_sigmoid, hidden, outputs = expert_forward(
        expert_rows, gate_mat, up_mat, down_mat
    )
    cot_recv, gate_recv = (
        lax.all_to_all(cot_send, "expert", split_axis=0, concat_axis=0, tiled=True),
        lax.all_to_all(gate_send, "expert", split_axis=0, concat_axis=0, tiled=True),
    )
    cot_rows = cot_recv.reshape(buffer_rows, model_width)
    gate_rows = gate_recv.reshape(buffer_rows).astype(jnp.float32)
    scaled = (gate_rows[:, None] * cot_rows.astype(jnp.float32)).astype(jnp.bfloat16)
    d_hidden = jnp.dot(scaled, down_mat, preferred_element_type=jnp.float32)
    d_pre_gate = (
        d_hidden * pre_up * gate_sigmoid * (1.0 + pre_gate * (1.0 - gate_sigmoid))
    ).astype(jnp.bfloat16)
    d_pre_up = (d_hidden * pre_gate * gate_sigmoid).astype(jnp.bfloat16)
    slot_grad = (
        jnp.dot(d_pre_gate, gate_mat, preferred_element_type=jnp.float32)
        + jnp.dot(d_pre_up, up_mat, preferred_element_type=jnp.float32)
    ).astype(jnp.bfloat16)
    pieces = []
    for operand, partner in ((d_pre_gate, expert_rows), (d_pre_up, expert_rows), (hidden, scaled)):
        pieces.append(rounded(contract_first(operand, partner)))
    summed = lax.psum_scatter(
        jnp.concatenate(pieces, axis=1).astype(jnp.bfloat16), "dp", scatter_dimension=0, tiled=True
    ).astype(jnp.float32)
    grad_gate = summed[:, :model_width].astype(jnp.bfloat16)[None]
    grad_up = summed[:, model_width : 2 * model_width].astype(jnp.bfloat16)[None]
    grad_down_t = summed[:, 2 * model_width :].astype(jnp.bfloat16)[None]
    slot_back = slot_grad.reshape(experts, capacity, model_width)
    out_send = outputs.reshape(experts, capacity, model_width)
    grad_back, out_back = (
        lax.all_to_all(slot_back, "expert", split_axis=0, concat_axis=0, tiled=True),
        lax.all_to_all(out_send, "expert", split_axis=0, concat_axis=0, tiled=True),
    )
    picked = out_back.reshape(buffer_rows, model_width)[position].astype(jnp.float32)
    picked = picked.reshape(tok_rows, top_count, model_width)
    gate_grad = jnp.sum(picked * cotangent.astype(jnp.float32)[:, None, :], axis=2).astype(
        jnp.bfloat16
    )
    gathered = grad_back.reshape(buffer_rows, model_width)[position].astype(jnp.float32)
    token_grad = gathered.reshape(tok_rows, top_count, model_width).sum(axis=1).astype(jnp.bfloat16)
    return (token_grad, gate_grad, grad_gate, grad_up, grad_down_t)


def swap(value, flip):
    count = lax.axis_size(BOTH)
    return lax.ppermute(value, BOTH, [(i, i ^ flip) for i in range(count)])


def added(*terms):
    return sum(term.astype(jnp.float32) for term in terms).astype(jnp.bfloat16)


def tied(*values):
    return lax.optimization_barrier(values)


def kernel_params(flops, moved, transcendentals=0, megabytes=14):
    return {
        "compiler_params": pltpu.CompilerParams(vmem_limit_bytes=megabytes * 1024 * 1024),
        "cost_estimate": pl.CostEstimate(
            flops=flops, bytes_accessed=moved, transcendentals=transcendentals
        ),
    }


IN_HBM = pl.BlockSpec(memory_space=pl.ANY)
IN_VMEM = pl.BlockSpec(memory_space=pltpu.VMEM)
IN_SMEM = pl.BlockSpec(memory_space=pltpu.SMEM)


def kept(value):
    return pltpu.with_memory_space_constraint(value, pltpu.VMEM)


def left_out(value):
    return pltpu.with_memory_space_constraint(value, pltpu.HBM)


def fetched(pairs, sems):
    copies = [pltpu.make_async_copy(src, dst, sems.at[i]) for i, (src, dst) in enumerate(pairs)]
    for copy in copies:
        copy.start()
    return copies


def placed(pieces, target):
    pairs, first = [], 0
    for piece in pieces:
        pairs.append((piece, target.at[pl.ds(first, piece.shape[0])]))
        first += piece.shape[0]
    return pairs


def as_cotangents(x_refs):
    views = []
    for column, near in (x_refs[:2], x_refs[2:]):
        block = column.shape[0] // 4
        views += [column.at[pl.ds(0, 2 * block)], near.at[pl.ds(0, block)]]
        views += [column.at[pl.ds(2 * block, 2 * block)], near.at[pl.ds(block, 3 * block)]]
    return views


def forward_kernel(*refs):
    pieces, weight_refs, weight_outs, sems = refs[:4], refs[4:7], refs[7:10], refs[-1]
    rows_out, slope_out, swish_out, hidden_out = refs[10:14]
    units = slope_out.shape[1]
    pairs = placed(pieces, rows_out)
    for start in range(0, units, TILE):
        for i in range(2):
            rows = pl.ds(start, TILE)
            pairs.append((weight_refs[i].at[0, rows], weight_outs[i].at[rows]))
    half = weight_outs[2].shape[0] // 2
    for i in range(2):
        rows = pl.ds(i * half, half)
        pairs.append((weight_refs[2].at[0, rows], weight_outs[2].at[rows]))
    copies = fetched(pairs, sems)
    for copy in copies[:4]:
        copy.wait()
    for step, start in enumerate(range(0, units, TILE)):
        for copy in copies[4 + 2 * step : 6 + 2 * step]:
            copy.wait()
        rows = rows_out[...]
        chunk = slice(start, start + TILE)
        pre_gate = contract_last(rows, weight_outs[0][chunk])
        pre_up = contract_last(rows, weight_outs[1][chunk])
        gate_sigmoid = jax.nn.sigmoid(pre_gate)
        swish = pre_gate * gate_sigmoid
        slope_out[:, chunk] = pre_up * gate_sigmoid * (1.0 + pre_gate * (1.0 - gate_sigmoid))
        swish_out[:, chunk] = swish
        hidden_out[:, chunk] = swish * pre_up
    for copy in copies[-2:]:
        copy.wait()


def forward(pieces, weights):
    _, units, width = weights[0].shape
    rows = sum(piece.shape[0] for piece in pieces)
    outs = [pltpu.VMEM((rows, units), jnp.float32)] * 3
    for shape in ((rows, width), (width, units), (units, width), (units, width)):
        outs.insert(0, pltpu.VMEM(shape, jnp.bfloat16))
    return pl.pallas_call(
        forward_kernel,
        in_specs=[IN_HBM] * 7,
        out_specs=[IN_VMEM] * 7,
        out_shape=outs,
        scratch_shapes=[pltpu.SemaphoreType.DMA((6 + 2 * (units // TILE),))],
        **kernel_params(4 * rows * units * width, 2 * rows * width, rows * units),
    )(*[left_out(value) for value in (*pieces, *weights)])


def backward_kernel(first, count, place_ref, *refs):
    pieces, (slope_ref, swish_ref, hidden_ref) = refs[:count], refs[count : count + 3]
    gate_ref, up_ref, down_ref, _ = refs[count + 3 : count + 7]
    parts_out, (rows_out, lefts_out, token_out, sems) = refs[count + 7 : -4], refs[-4:]
    width, units = down_ref.shape
    rows, packed = rows_out.shape
    copies = fetched(placed(pieces, rows_out), sems)
    token_out[...] = jnp.zeros_like(token_out)
    for copy in copies:
        copy.wait()
    saved = slice(first, first + rows)
    column = lax.broadcasted_iota(jnp.int32, (rows, packed - width), 1) == place_ref[0]
    table = rows_out[:, width:].astype(jnp.float32)
    gates = jnp.sum(jnp.where(column, table, 0.0), axis=1, keepdims=True)
    score = jnp.zeros((rows, 1), jnp.float32)
    for start in range(0, units, TILE):
        chunk = slice(start, start + TILE)
        raw = jnp.dot(
            rows_out[:, :width], down_ref[:, chunk], preferred_element_type=jnp.float32
        )
        hidden = hidden_ref[saved, chunk]
        score += jnp.sum(hidden * raw, axis=1, keepdims=True)
        d_hidden = gates * raw
        lefts_out[:, chunk] = (d_hidden * slope_ref[saved, chunk]).astype(jnp.bfloat16)
        lefts_out[:, units + start : units + start + TILE] = (
            d_hidden * swish_ref[saved, chunk]
        ).astype(jnp.bfloat16)
        lefts_out[:, 2 * units + start : 2 * units + start + TILE] = (gates * hidden).astype(
            jnp.bfloat16
        )
    scores = jnp.where(column, score, 0.0).astype(jnp.bfloat16)
    block = rows // count
    for i, part in enumerate(parts_out):
        part[:, width:] = scores[i * block : (i + 1) * block]
    for start in range(0, width, 2 * TILE):
        chunk = slice(start, start + 2 * TILE)
        total = (
            jnp.dot(lefts_out[:, :units], gate_ref[:, chunk], preferred_element_type=jnp.float32)
            + jnp.dot(
                lefts_out[:, units : 2 * units],
                up_ref[:, chunk],
                preferred_element_type=jnp.float32,
            )
        ).astype(jnp.bfloat16)
        for i, part in enumerate(parts_out):
            part[:, chunk] = total[i * block : (i + 1) * block]


def backward(place, pieces, saved, first, weights, after):
    units, width = weights[0].shape
    count = len(pieces)
    block, packed = pieces[0].shape
    rows = count * block
    return pl.pallas_call(
        functools.partial(backward_kernel, first, count),
        in_specs=[IN_SMEM] + [IN_HBM] * count + [IN_VMEM] * 6 + [IN_HBM],
        out_specs=[IN_VMEM] * (count + 3),
        out_shape=[jax.ShapeDtypeStruct((block, packed), jnp.bfloat16)] * count
        + [
            pltpu.VMEM((rows, packed), jnp.bfloat16),
            pltpu.VMEM((rows, 3 * units), jnp.bfloat16),
            jax.ShapeDtypeStruct((8, 128), jnp.float32),
        ],
        scratch_shapes=[pltpu.SemaphoreType.DMA((count,))],
        **kernel_params(0, 0),
    )(place, *pieces, *[kept(value) for value in (*saved, *weights)], after)


def own_gradient_kernel(place_ref, *refs):
    left_refs, x_ref, own_cot_refs = refs[:3], refs[3], refs[4:7]
    x_refs, weight_refs = refs[7:11], refs[11:13]
    outs, (slope_out, swish_out, hidden_out, token_out) = refs[13:16], refs[16:20]
    lefts, rows, gate_ref, up_ref, sems = refs[20:]
    share, tile = outs[0].shape
    units = left_refs[0].shape[1] // 3
    start = pl.multiple_of(place_ref[1] * share, 128)
    own = pl.ds(start, share)
    copies = [
        pltpu.make_async_copy(source, target, sems.at[i])
        for i, (source, target) in enumerate(
            placed(as_cotangents(x_refs), rows)
            + [(weight_refs[0].at[0, own], gate_ref), (weight_refs[1].at[0, own], up_ref)]
        )
    ]

    @pl.when(pl.program_id(0) == 0)
    def _():
        for copy in copies:
            copy.start()
        token_out[...] = jnp.zeros_like(token_out)
        for i in range(3):
            lefts[i] = jnp.concatenate(
                [ref[:, pl.ds(start + i * units, share)] for ref in left_refs], axis=0
            ).T

    chunk = pl.ds(pl.multiple_of(pl.program_id(0) * tile, tile), tile)
    cot_rows = jnp.concatenate([ref[:, chunk] for ref in own_cot_refs], axis=0)
    for i, right in enumerate((x_ref[:, chunk], x_ref[:, chunk], cot_rows)):
        outs[i][...] = jnp.dot(lefts[i], right, preferred_element_type=jnp.float32).astype(
            jnp.bfloat16
        )

    @pl.when(pl.program_id(0) == pl.num_programs(0) - 1)
    def _():
        for copy in copies:
            copy.wait()
        pre_gate = contract_last(gate_ref[...], rows[...])
        pre_up = contract_last(up_ref[...], rows[...])
        gate_sigmoid = jax.nn.sigmoid(pre_gate)
        swish = pre_gate * gate_sigmoid
        slope_out[...] = (pre_up * gate_sigmoid * (1.0 + pre_gate * (1.0 - gate_sigmoid))).astype(
            jnp.bfloat16
        )
        swish_out[...] = swish.astype(jnp.bfloat16)
        hidden_out[...] = (swish * pre_up).astype(jnp.bfloat16)


def own_gradients(place, lefts, x_rows, cot_rows, x_away, weights, share):
    rows, width = x_rows.shape
    tile = 2 * TILE
    half = pltpu.VMEM((share, width), jnp.bfloat16)
    return pl.pallas_call(
        own_gradient_kernel,
        grid=(width // tile,),
        in_specs=[IN_SMEM] + [IN_VMEM] * 7 + [IN_HBM] * 6,
        out_specs=[pl.BlockSpec((share, tile), lambda i: (0, i))] * 3
        + [pl.BlockSpec((share, rows), lambda i: (0, 0))] * 3
        + [pl.BlockSpec((8, 128), lambda i: (0, 0))],
        out_shape=[jax.ShapeDtypeStruct((share, width), jnp.bfloat16)] * 3
        + [jax.ShapeDtypeStruct((share, rows), jnp.bfloat16)] * 3
        + [jax.ShapeDtypeStruct((8, 128), jnp.float32)],
        scratch_shapes=[
            pltpu.VMEM((3, share, rows), jnp.bfloat16),
            pltpu.VMEM((rows, width), jnp.bfloat16),
            half,
            half,
            pltpu.SemaphoreType.DMA((10,)),
        ],
        **kernel_params(0, 0, 0, 24),
    )(
        place,
        *[kept(value) for value in (*lefts, x_rows, *cot_rows)],
        *[left_out(value) for value in (*x_away, *weights)],
    )


def whole_gradient_kernel(place_ref, *refs):
    cot_refs, down_ref, saved_refs, x_refs = refs[:6], refs[6], refs[7:10], refs[10:14]
    own_refs, outs = refs[14:17], refs[18:21]
    rows, cot, down, slope, swish, hidden, lefts, sems = refs[21:]
    share, tile = outs[0].shape[1:]
    width = rows.shape[1]

    @pl.when(pl.program_id(0) == 0)
    def _():
        own = pl.ds(pl.multiple_of(place_ref[1] * share, 128), share)
        copies = fetched(
            placed(cot_refs, cot)
            + [(down_ref.at[0, :, own], down)]
            + list(zip(saved_refs, (slope, swish, hidden)))
            + placed(as_cotangents(x_refs), rows),
            sems,
        )
        for copy in copies[:7]:
            copy.wait()
        table = cot[:, width:]
        pick = (lax.broadcasted_iota(jnp.int32, (16, table.shape[1]), 1) == place_ref[0]).astype(
            jnp.bfloat16
        )
        gates = contract_last(pick, table)[:1]
        raw = jnp.dot(cot[:, :width], down[...], preferred_element_type=jnp.float32).T
        d_hidden = gates * raw
        for copy in copies[7:10]:
            copy.wait()
        for i, factor in enumerate((slope, swish)):
            lefts[i] = (d_hidden * factor[...].astype(jnp.float32)).astype(jnp.bfloat16)
        lefts[2] = (gates * hidden[...].astype(jnp.float32)).astype(jnp.bfloat16)
        for copy in copies[10:]:
            copy.wait()

    first = pl.multiple_of(pl.program_id(0) * tile, tile)
    for i in range(3):
        right = rows if i < 2 else cot
        away = jnp.dot(lefts[i], right[:, pl.ds(first, tile)], preferred_element_type=jnp.float32)
        outs[i][0] = (own_refs[i][...].astype(jnp.float32) + away).astype(jnp.bfloat16)


def whole_gradients(place, cot_rows, w_down, saved, x_rows, own, after):
    share, width = own[0].shape
    tile = 2 * TILE
    rows = sum(piece.shape[0] for piece in x_rows)
    half = pltpu.VMEM((share, rows), jnp.bfloat16)
    return pl.pallas_call(
        whole_gradient_kernel,
        grid=(width // tile,),
        in_specs=[IN_SMEM]
        + [IN_HBM] * 14
        + [pl.BlockSpec((share, tile), lambda i: (0, i))] * 3
        + [IN_HBM],
        out_specs=[pl.BlockSpec((1, share, tile), lambda i: (0, 0, i))] * 3,
        out_shape=[jax.ShapeDtypeStruct((1, share, width), jnp.bfloat16)] * 3,
        scratch_shapes=[
            pltpu.VMEM((rows, width), jnp.bfloat16),
            pltpu.VMEM((rows, cot_rows[0].shape[1]), jnp.bfloat16),
            pltpu.VMEM((width, share), jnp.bfloat16),
            half,
            half,
            half,
            pltpu.VMEM((3, share, rows), jnp.bfloat16),
            pltpu.SemaphoreType.DMA((18,)),
        ],
        **kernel_params(
            8 * rows * share * width, 4 * rows * width + 12 * share * width, rows * share, 32
        ),
    )(
        place,
        *[left_out(value) for value in cot_rows[:-1]],
        cot_rows[-1],
        left_out(w_down),
        *saved,
        *[left_out(value) for value in x_rows],
        *own,
        after,
    )


def finish_kernel(*refs):
    part_refs, ids_ref, (token_out, gate_out) = refs[:-3], refs[-3], refs[-2:]
    rows, width = token_out.shape
    lanes = part_refs[0].shape[1] - width
    token_out[...] = added(*[ref[:, :width] for ref in part_refs])
    scores = added(*[ref[:, width:] for ref in part_refs]).astype(jnp.float32)
    scores = jnp.concatenate([scores, jnp.zeros((lanes - rows, lanes), jnp.float32)], axis=0).T
    expert = lax.broadcasted_iota(jnp.int32, (lanes, rows), 0)
    named = [
        jnp.sum(
            jnp.where(ids_ref[k : k + 1] == expert, scores[:, :rows], 0.0), axis=0, keepdims=True
        )
        for k in range(ids_ref.shape[0])
    ]
    gate_out[...] = jnp.concatenate(named, axis=0).astype(jnp.bfloat16)


def finished(parts, ids, width):
    top, rows = ids.shape
    packed = parts[0].shape[1]
    return pl.pallas_call(
        finish_kernel,
        grid=(1,),
        in_specs=[pl.BlockSpec((rows, packed), lambda i: (0, 0))] * len(parts)
        + [pl.BlockSpec((top, rows), lambda i: (0, 0))],
        out_specs=[
            pl.BlockSpec((rows, width), lambda i: (0, 0)),
            pl.BlockSpec((top, rows), lambda i: (0, 0)),
        ],
        out_shape=[
            jax.ShapeDtypeStruct((rows, width), jnp.bfloat16),
            jax.ShapeDtypeStruct((top, rows), jnp.bfloat16),
        ],
        **kernel_params(0, 0, 0, 8),
    )(*parts, ids)


def dense_body(tokens, expert_ids, gate_weights, cotangent, w_gate, w_up, w_down):
    model_width = tokens.shape[1]
    experts = lax.axis_size("expert")
    groups = lax.axis_size("dp")
    share = w_gate.shape[1] // groups
    place = jnp.stack([lax.axis_index("expert"), lax.axis_index("dp")]).astype(jnp.int32)
    group, core, near, low, high = 1, 2, 4, 8, 16
    lanes = -(-experts // 128) * 128
    named = expert_ids.T[:, :, None] == jnp.arange(lanes, dtype=jnp.int32)[None, None, :]
    gate_table = jnp.sum(
        jnp.where(named, gate_weights.T.astype(jnp.float32)[:, :, None], 0.0), axis=0
    ).astype(jnp.bfloat16)

    def column_of(value):
        return [swap(value, high), swap(value, low), swap(value, low | high)]

    weights = (w_gate, w_up, w_down)
    packed = jnp.concatenate([cotangent, gate_table], axis=1)
    x_high, x_low, x_both = column_of(tokens)
    packed, x_low = tied(packed, x_low)
    cot_mine_away, near_mine_away = swap(packed, group), swap(packed, group | near)
    packed, cot_mine_away, near_mine_away, x_high, x_low, x_both = tied(
        packed, cot_mine_away, near_mine_away, x_high, x_low, x_both
    )
    x_column = jnp.concatenate([tokens, x_high, x_low, x_both], axis=0)
    x_near = swap(x_column, near)
    x_column_away = swap(x_column, group)
    *cot_far, x_near, x_column_away = tied(*column_of(packed), x_near, x_column_away)
    x_near_away = swap(x_near, group)
    cot_column = jnp.concatenate([packed, *cot_far], axis=0)
    cot_high_away = swap(cot_mine_away, high)
    cot_near = swap(cot_column, near)
    *kept_weights, x_rows, slope, swish, hidden = forward(
        [x_column, swap(x_column, core), x_near, swap(x_near, core)], weights
    )
    saved = (slope, swish, hidden)
    own_part, other_part, column_cot, column_lefts, token = backward(
        place, [cot_column, swap(cot_column, core)], saved, 0, kept_weights, place
    )
    column_own, column_given = own_part, swap(other_part, core)
    x_column_other = swap(x_column_away, core)
    cot_near, token, x_near_away, x_column_other, cot_high_away = tied(
        cot_near, token, x_near_away, x_column_other, cot_high_away
    )
    cot_first_away = jnp.concatenate([cot_mine_away, cot_high_away], axis=0)
    cot_second_away, cot_first_other = swap(cot_first_away, low), swap(cot_first_away, core)
    x_near_other = swap(x_near_away, core)
    near_mine_other = swap(near_mine_away, core)
    near_far_away = swap(cot_near[packed.shape[0] :], group)
    half = x_rows.shape[0] // 2
    other_part, other_cot, other_lefts, _ = backward(
        place, [swap(cot_near, core)], saved, half + half // 2, kept_weights, token
    )
    own_part, own_cot, own_lefts, _ = backward(
        place, [cot_near], saved, half, kept_weights, token
    )
    other_part, x_near_other, column_given, cot_first_other, near_mine_other = tied(
        other_part, x_near_other, column_given, cot_first_other, near_mine_other
    )
    near_sum = added(own_part, swap(other_part, core))
    partial = added(column_own, column_given, swap(near_sum, near))
    block = packed.shape[0]
    x_away = [x_column_away, x_near_away, x_column_other, x_near_other]
    *own, slope, swish, hidden, token = own_gradients(
        place,
        [column_lefts, own_lefts, other_lefts],
        x_rows,
        [column_cot, own_cot, other_cot],
        x_away,
        weights[:2],
        share,
    )
    cot_second_away, near_far_away, partial, token = tied(
        cot_second_away, near_far_away, partial, token
    )
    cot_rest_away = jnp.concatenate([cot_second_away, near_far_away], axis=0)
    cot_away = [cot_first_away, near_mine_away, cot_rest_away]
    cot_away += [cot_first_other, near_mine_other, swap(cot_rest_away, core)]
    saved = (slope, swish, hidden)
    grads = list(whole_gradients(place, cot_away, w_down, saved, x_away, own, token))
    parts = [
        partial,
        swap(partial[block : 2 * block], high),
        swap(partial[2 * block : 3 * block], low),
        swap(partial[3 * block :], low | high),
    ]
    *parts, grads[0] = tied(*parts, grads[0])
    token_grad, gate_grad = finished(parts, expert_ids.T, model_width)
    return (token_grad, gate_grad.T, *grads)


def body(tokens, expert_ids, *rest):
    tok_rows, top_count = expert_ids.shape
    if 2 * tok_rows * top_count // lax.axis_size("expert") < tok_rows:
        return routed_body(tokens, expert_ids, *rest)
    return dense_body(tokens, expert_ids, *rest)


def solution(mesh):
    return jax.shard_map(
        body,
        mesh=mesh,
        in_specs=(
            P(("expert", "dp"), None),
            P(("expert", "dp"), None),
            P(("expert", "dp"), None),
            P(("expert", "dp"), None),
            P("expert", None, None),
            P("expert", None, None),
            P("expert", None, None),
        ),
        out_specs=(
            P(("expert", "dp"), None),
            P(("expert", "dp"), None),
            P("expert", "dp", None),
            P("expert", "dp", None),
            P("expert", "dp", None),
        ),
        check_vma=False,
    )
```

```python
import functools

import jax
import jax.numpy as jnp
from jax import lax
from jax.experimental import pallas as pl
from jax.experimental.pallas import tpu as pltpu
from jax.sharding import PartitionSpec as P

TILE = 256
BOTH = ("expert", "dp")


def contract_last(left, right):
    return lax.dot_general(
        left, right, (((1,), (1,)), ((), ())), preferred_element_type=jnp.float32
    )


def contract_first(left, right):
    return lax.dot_general(
        left, right, (((0,), (0,)), ((), ())), preferred_element_type=jnp.float32
    )


def rounded(value):
    return lax.optimization_barrier(value.astype(jnp.bfloat16)).astype(jnp.float32)


def expert_forward(expert_rows, gate_mat, up_mat, down_mat):
    pre_gate = contract_last(expert_rows, gate_mat)
    pre_up = contract_last(expert_rows, up_mat)
    gate_sigmoid = jax.nn.sigmoid(pre_gate)
    hidden = (pre_gate * gate_sigmoid * pre_up).astype(jnp.bfloat16)
    outputs = contract_last(hidden, down_mat).astype(jnp.bfloat16)
    return (pre_gate, pre_up, gate_sigmoid, hidden, outputs)


def routed_body(tokens, expert_ids, gate_weights, cotangent, w_gate, w_up, w_down):
    tok_rows, top_count = expert_ids.shape
    model_width = tokens.shape[1]
    experts = lax.axis_size("expert")
    capacity = min(tok_rows, 2 * tok_rows * top_count // experts)
    slot_count = tok_rows * top_count
    buffer_rows = experts * capacity
    flat_ids = expert_ids.reshape(slot_count)
    onehot = (flat_ids[:, None] == jnp.arange(experts, dtype=jnp.int32)[None, :]).astype(jnp.int32)
    slot_rank = jnp.sum((jnp.cumsum(onehot, axis=0) - 1) * onehot, axis=1)
    position = flat_ids * capacity + slot_rank
    placing = (jnp.arange(buffer_rows, dtype=jnp.int32)[:, None] == position[None, :]).astype(
        jnp.bfloat16
    )
    token_map = placing.reshape(buffer_rows, tok_rows, top_count).sum(axis=2)
    x_send = jnp.dot(token_map, tokens, preferred_element_type=jnp.float32).astype(jnp.bfloat16)
    x_send = x_send.reshape(experts, capacity, model_width)
    cot_send = jnp.dot(token_map, cotangent, preferred_element_type=jnp.float32).astype(
        jnp.bfloat16
    )
    cot_send = cot_send.reshape(experts, capacity, model_width)
    gate_send = jnp.dot(
        placing, gate_weights.reshape(slot_count), preferred_element_type=jnp.float32
    )
    gate_send = gate_send.astype(jnp.bfloat16).reshape(experts, capacity)
    gate_mat = w_gate[0]
    up_mat = w_up[0]
    down_mat = w_down[0]
    x_recv = lax.all_to_all(x_send, "expert", split_axis=0, concat_axis=0, tiled=True)
    expert_rows = x_recv.reshape(buffer_rows, model_width)
    pre_gate, pre_up, gate_sigmoid, hidden, outputs = expert_forward(
        expert_rows, gate_mat, up_mat, down_mat
    )
    cot_recv, gate_recv = (
        lax.all_to_all(cot_send, "expert", split_axis=0, concat_axis=0, tiled=True),
        lax.all_to_all(gate_send, "expert", split_axis=0, concat_axis=0, tiled=True),
    )
    cot_rows = cot_recv.reshape(buffer_rows, model_width)
    gate_rows = gate_recv.reshape(buffer_rows).astype(jnp.float32)
    scaled = (gate_rows[:, None] * cot_rows.astype(jnp.float32)).astype(jnp.bfloat16)
    d_hidden = jnp.dot(scaled, down_mat, preferred_element_type=jnp.float32)
    d_pre_gate = (
        d_hidden * pre_up * gate_sigmoid * (1.0 + pre_gate * (1.0 - gate_sigmoid))
    ).astype(jnp.bfloat16)
    d_pre_up = (d_hidden * pre_gate * gate_sigmoid).astype(jnp.bfloat16)
    slot_grad = (
        jnp.dot(d_pre_gate, gate_mat, preferred_element_type=jnp.float32)
        + jnp.dot(d_pre_up, up_mat, preferred_element_type=jnp.float32)
    ).astype(jnp.bfloat16)
    pieces = []
    for operand, partner in ((d_pre_gate, expert_rows), (d_pre_up, expert_rows), (hidden, scaled)):
        pieces.append(rounded(contract_first(operand, partner)))
    summed = lax.psum_scatter(
        jnp.concatenate(pieces, axis=1).astype(jnp.bfloat16), "dp", scatter_dimension=0, tiled=True
    ).astype(jnp.float32)
    grad_gate = summed[:, :model_width].astype(jnp.bfloat16)[None]
    grad_up = summed[:, model_width : 2 * model_width].astype(jnp.bfloat16)[None]
    grad_down_t = summed[:, 2 * model_width :].astype(jnp.bfloat16)[None]
    slot_back = slot_grad.reshape(experts, capacity, model_width)
    out_send = outputs.reshape(experts, capacity, model_width)
    grad_back, out_back = (
        lax.all_to_all(slot_back, "expert", split_axis=0, concat_axis=0, tiled=True),
        lax.all_to_all(out_send, "expert", split_axis=0, concat_axis=0, tiled=True),
    )
    picked = out_back.reshape(buffer_rows, model_width)[position].astype(jnp.float32)
    picked = picked.reshape(tok_rows, top_count, model_width)
    gate_grad = jnp.sum(picked * cotangent.astype(jnp.float32)[:, None, :], axis=2).astype(
        jnp.bfloat16
    )
    gathered = grad_back.reshape(buffer_rows, model_width)[position].astype(jnp.float32)
    token_grad = gathered.reshape(tok_rows, top_count, model_width).sum(axis=1).astype(jnp.bfloat16)
    return (token_grad, gate_grad, grad_gate, grad_up, grad_down_t)


def swap(value, flip):
    count = lax.axis_size(BOTH)
    return lax.ppermute(value, BOTH, [(i, i ^ flip) for i in range(count)])


def added(*terms):
    return sum(term.astype(jnp.float32) for term in terms).astype(jnp.bfloat16)


def tied(*values):
    return lax.optimization_barrier(values)


def kernel_params(flops, moved, transcendentals=0, megabytes=14):
    return {
        "compiler_params": pltpu.CompilerParams(vmem_limit_bytes=megabytes * 1024 * 1024),
        "cost_estimate": pl.CostEstimate(
            flops=flops, bytes_accessed=moved, transcendentals=transcendentals
        ),
    }


IN_HBM = pl.BlockSpec(memory_space=pl.ANY)
IN_VMEM = pl.BlockSpec(memory_space=pltpu.VMEM)
IN_SMEM = pl.BlockSpec(memory_space=pltpu.SMEM)


def kept(value):
    return pltpu.with_memory_space_constraint(value, pltpu.VMEM)


def left_out(value):
    return pltpu.with_memory_space_constraint(value, pltpu.HBM)


def fetched(pairs, sems):
    copies = [pltpu.make_async_copy(src, dst, sems.at[i]) for i, (src, dst) in enumerate(pairs)]
    for copy in copies:
        copy.start()
    return copies


def placed(pieces, target):
    pairs, first = [], 0
    for piece in pieces:
        pairs.append((piece, target.at[pl.ds(first, piece.shape[0])]))
        first += piece.shape[0]
    return pairs


def as_cotangents(x_refs):
    views = []
    for column, near in (x_refs[:2], x_refs[2:]):
        block = column.shape[0] // 4
        views += [column.at[pl.ds(0, 2 * block)], near.at[pl.ds(0, block)]]
        views += [column.at[pl.ds(2 * block, 2 * block)], near.at[pl.ds(block, 3 * block)]]
    return views


def forward_kernel(*refs):
    pieces, weight_refs, weight_outs, sems = refs[:4], refs[4:7], refs[7:10], refs[-1]
    rows_out, slope_out, swish_out, hidden_out = refs[10:14]
    units = slope_out.shape[1]
    pairs = placed(pieces, rows_out)
    for start in range(0, units, TILE):
        for i in range(2):
            rows = pl.ds(start, TILE)
            pairs.append((weight_refs[i].at[0, rows], weight_outs[i].at[rows]))
    half = weight_outs[2].shape[0] // 2
    for i in range(2):
        rows = pl.ds(i * half, half)
        pairs.append((weight_refs[2].at[0, rows], weight_outs[2].at[rows]))
    copies = fetched(pairs, sems)
    for copy in copies[:4]:
        copy.wait()
    for step, start in enumerate(range(0, units, TILE)):
        for copy in copies[4 + 2 * step : 6 + 2 * step]:
            copy.wait()
        rows = rows_out[...]
        chunk = slice(start, start + TILE)
        pre_gate = contract_last(rows, weight_outs[0][chunk])
        pre_up = contract_last(rows, weight_outs[1][chunk])
        gate_sigmoid = jax.nn.sigmoid(pre_gate)
        swish = pre_gate * gate_sigmoid
        slope_out[:, chunk] = pre_up * gate_sigmoid * (1.0 + pre_gate * (1.0 - gate_sigmoid))
        swish_out[:, chunk] = swish
        hidden_out[:, chunk] = swish * pre_up
    for copy in copies[-2:]:
        copy.wait()


def forward(pieces, weights):
    _, units, width = weights[0].shape
    rows = sum(piece.shape[0] for piece in pieces)
    outs = [pltpu.VMEM((rows, units), jnp.float32)] * 3
    for shape in ((rows, width), (width, units), (units, width), (units, width)):
        outs.insert(0, pltpu.VMEM(shape, jnp.bfloat16))
    return pl.pallas_call(
        forward_kernel,
        in_specs=[IN_HBM] * 7,
        out_specs=[IN_VMEM] * 7,
        out_shape=outs,
        scratch_shapes=[pltpu.SemaphoreType.DMA((6 + 2 * (units // TILE),))],
        **kernel_params(4 * rows * units * width, 2 * rows * width, rows * units),
    )(*[left_out(value) for value in (*pieces, *weights)])


def backward_kernel(first, count, place_ref, *refs):
    pieces, (slope_ref, swish_ref, hidden_ref) = refs[:count], refs[count : count + 3]
    gate_ref, up_ref, down_ref, _ = refs[count + 3 : count + 7]
    parts_out, (rows_out, lefts_out, token_out, sems) = refs[count + 7 : -4], refs[-4:]
    width, units = down_ref.shape
    rows, packed = rows_out.shape
    copies = fetched(placed(pieces, rows_out), sems)
    token_out[...] = jnp.zeros_like(token_out)
    for copy in copies:
        copy.wait()
    saved = slice(first, first + rows)
    column = lax.broadcasted_iota(jnp.int32, (rows, packed - width), 1) == place_ref[0]
    table = rows_out[:, width:].astype(jnp.float32)
    gates = jnp.sum(jnp.where(column, table, 0.0), axis=1, keepdims=True)
    score = jnp.zeros((rows, 1), jnp.float32)
    for start in range(0, units, TILE):
        chunk = slice(start, start + TILE)
        raw = jnp.dot(
            rows_out[:, :width], down_ref[:, chunk], preferred_element_type=jnp.float32
        )
        hidden = hidden_ref[saved, chunk]
        score += jnp.sum(hidden * raw, axis=1, keepdims=True)
        d_hidden = gates * raw
        lefts_out[:, chunk] = (d_hidden * slope_ref[saved, chunk]).astype(jnp.bfloat16)
        lefts_out[:, units + start : units + start + TILE] = (
            d_hidden * swish_ref[saved, chunk]
        ).astype(jnp.bfloat16)
        lefts_out[:, 2 * units + start : 2 * units + start + TILE] = (gates * hidden).astype(
            jnp.bfloat16
        )
    scores = jnp.where(column, score, 0.0).astype(jnp.bfloat16)
    block = rows // count
    for i, part in enumerate(parts_out):
        part[:, width:] = scores[i * block : (i + 1) * block]
    for start in range(0, width, 2 * TILE):
        chunk = slice(start, start + 2 * TILE)
        total = (
            jnp.dot(lefts_out[:, :units], gate_ref[:, chunk], preferred_element_type=jnp.float32)
            + jnp.dot(
                lefts_out[:, units : 2 * units],
                up_ref[:, chunk],
                preferred_element_type=jnp.float32,
            )
        ).astype(jnp.bfloat16)
        for i, part in enumerate(parts_out):
            part[:, chunk] = total[i * block : (i + 1) * block]


def backward(place, pieces, saved, first, weights, after):
    units, width = weights[0].shape
    count = len(pieces)
    block, packed = pieces[0].shape
    rows = count * block
    return pl.pallas_call(
        functools.partial(backward_kernel, first, count),
        in_specs=[IN_SMEM] + [IN_HBM] * count + [IN_VMEM] * 6 + [IN_HBM],
        out_specs=[IN_VMEM] * (count + 3),
        out_shape=[jax.ShapeDtypeStruct((block, packed), jnp.bfloat16)] * count
        + [
            pltpu.VMEM((rows, packed), jnp.bfloat16),
            pltpu.VMEM((rows, 3 * units), jnp.bfloat16),
            jax.ShapeDtypeStruct((8, 128), jnp.float32),
        ],
        scratch_shapes=[pltpu.SemaphoreType.DMA((count,))],
        **kernel_params(0, 0),
    )(place, *pieces, *[kept(value) for value in (*saved, *weights)], after)


def own_gradient_kernel(place_ref, *refs):
    left_refs, x_ref, own_cot_refs = refs[:3], refs[3], refs[4:7]
    x_refs, weight_refs = refs[7:11], refs[11:13]
    outs, (slope_out, swish_out, hidden_out, token_out) = refs[13:16], refs[16:20]
    lefts, rows, gate_ref, up_ref, sems = refs[20:]
    share, tile = outs[0].shape
    units = left_refs[0].shape[1] // 3
    start = pl.multiple_of(place_ref[1] * share, 128)
    own = pl.ds(start, share)
    copies = [
        pltpu.make_async_copy(source, target, sems.at[i])
        for i, (source, target) in enumerate(
            placed(as_cotangents(x_refs), rows)
            + [(weight_refs[0].at[0, own], gate_ref), (weight_refs[1].at[0, own], up_ref)]
        )
    ]

    @pl.when(pl.program_id(0) == 0)
    def _():
        for copy in copies:
            copy.start()
        token_out[...] = jnp.zeros_like(token_out)
        for i in range(3):
            lefts[i] = jnp.concatenate(
                [ref[:, pl.ds(start + i * units, share)] for ref in left_refs], axis=0
            ).T

    chunk = pl.ds(pl.multiple_of(pl.program_id(0) * tile, tile), tile)
    cot_rows = jnp.concatenate([ref[:, chunk] for ref in own_cot_refs], axis=0)
    for i, right in enumerate((x_ref[:, chunk], x_ref[:, chunk], cot_rows)):
        outs[i][...] = jnp.dot(lefts[i], right, preferred_element_type=jnp.float32).astype(
            jnp.bfloat16
        )

    @pl.when(pl.program_id(0) == pl.num_programs(0) - 1)
    def _():
        for copy in copies:
            copy.wait()
        pre_gate = contract_last(gate_ref[...], rows[...])
        pre_up = contract_last(up_ref[...], rows[...])
        gate_sigmoid = jax.nn.sigmoid(pre_gate)
        swish = pre_gate * gate_sigmoid
        slope_out[...] = (pre_up * gate_sigmoid * (1.0 + pre_gate * (1.0 - gate_sigmoid))).astype(
            jnp.bfloat16
        )
        swish_out[...] = swish.astype(jnp.bfloat16)
        hidden_out[...] = (swish * pre_up).astype(jnp.bfloat16)


def own_gradients(place, lefts, x_rows, cot_rows, x_away, weights, share):
    rows, width = x_rows.shape
    tile = 2 * TILE
    half = pltpu.VMEM((share, width), jnp.bfloat16)
    return pl.pallas_call(
        own_gradient_kernel,
        grid=(width // tile,),
        in_specs=[IN_SMEM] + [IN_VMEM] * 7 + [IN_HBM] * 6,
        out_specs=[pl.BlockSpec((share, tile), lambda i: (0, i))] * 3
        + [pl.BlockSpec((share, rows), lambda i: (0, 0))] * 3
        + [pl.BlockSpec((8, 128), lambda i: (0, 0))],
        out_shape=[jax.ShapeDtypeStruct((share, width), jnp.bfloat16)] * 3
        + [jax.ShapeDtypeStruct((share, rows), jnp.bfloat16)] * 3
        + [jax.ShapeDtypeStruct((8, 128), jnp.float32)],
        scratch_shapes=[
            pltpu.VMEM((3, share, rows), jnp.bfloat16),
            pltpu.VMEM((rows, width), jnp.bfloat16),
            half,
            half,
            pltpu.SemaphoreType.DMA((10,)),
        ],
        **kernel_params(0, 0, 0, 24),
    )(
        place,
        *[kept(value) for value in (*lefts, x_rows, *cot_rows)],
        *[left_out(value) for value in (*x_away, *weights)],
    )


def whole_gradient_kernel(place_ref, *refs):
    cot_refs, down_ref, saved_refs, x_refs = refs[:6], refs[6], refs[7:10], refs[10:14]
    own_refs, outs = refs[14:17], refs[18:21]
    rows, cot, down, slope, swish, hidden, lefts, sems = refs[21:]
    share, tile = outs[0].shape[1:]
    width = rows.shape[1]

    @pl.when(pl.program_id(0) == 0)
    def _():
        own = pl.ds(pl.multiple_of(place_ref[1] * share, 128), share)
        copies = fetched(
            placed(cot_refs, cot)
            + [(down_ref.at[0, :, own], down)]
            + list(zip(saved_refs, (slope, swish, hidden)))
            + placed(as_cotangents(x_refs), rows),
            sems,
        )
        for copy in copies[:7]:
            copy.wait()
        table = cot[:, width:]
        pick = (lax.broadcasted_iota(jnp.int32, (16, table.shape[1]), 1) == place_ref[0]).astype(
            jnp.bfloat16
        )
        gates = contract_last(pick, table)[:1]
        raw = jnp.dot(cot[:, :width], down[...], preferred_element_type=jnp.float32).T
        d_hidden = gates * raw
        for copy in copies[7:10]:
            copy.wait()
        for i, factor in enumerate((slope, swish)):
            lefts[i] = (d_hidden * factor[...].astype(jnp.float32)).astype(jnp.bfloat16)
        lefts[2] = (gates * hidden[...].astype(jnp.float32)).astype(jnp.bfloat16)
        for copy in copies[10:]:
            copy.wait()

    first = pl.multiple_of(pl.program_id(0) * tile, tile)
    for i in range(3):
        right = rows if i < 2 else cot
        away = jnp.dot(lefts[i], right[:, pl.ds(first, tile)], preferred_element_type=jnp.float32)
        outs[i][0] = (own_refs[i][...].astype(jnp.float32) + away).astype(jnp.bfloat16)


def whole_gradients(place, cot_rows, w_down, saved, x_rows, own, after):
    share, width = own[0].shape
    tile = 4 * TILE
    rows = sum(piece.shape[0] for piece in x_rows)
    half = pltpu.VMEM((share, rows), jnp.bfloat16)
    return pl.pallas_call(
        whole_gradient_kernel,
        grid=(width // tile,),
        in_specs=[IN_SMEM]
        + [IN_HBM] * 14
        + [pl.BlockSpec((share, tile), lambda i: (0, i))] * 3
        + [IN_HBM],
        out_specs=[pl.BlockSpec((1, share, tile), lambda i: (0, 0, i))] * 3,
        out_shape=[jax.ShapeDtypeStruct((1, share, width), jnp.bfloat16)] * 3,
        scratch_shapes=[
            pltpu.VMEM((rows, width), jnp.bfloat16),
            pltpu.VMEM((rows, cot_rows[0].shape[1]), jnp.bfloat16),
            pltpu.VMEM((width, share), jnp.bfloat16),
            half,
            half,
            half,
            pltpu.VMEM((3, share, rows), jnp.bfloat16),
            pltpu.SemaphoreType.DMA((18,)),
        ],
        **kernel_params(
            8 * rows * share * width, 4 * rows * width + 12 * share * width, rows * share, 32
        ),
    )(
        place,
        *[left_out(value) for value in cot_rows[:-1]],
        cot_rows[-1],
        left_out(w_down),
        *saved,
        *[left_out(value) for value in x_rows],
        *own,
        after,
    )


def finish_kernel(*refs):
    part_refs, ids_ref, (token_out, gate_out) = refs[:-3], refs[-3], refs[-2:]
    rows, width = token_out.shape
    lanes = part_refs[0].shape[1] - width
    token_out[...] = added(*[ref[:, :width] for ref in part_refs])
    scores = added(*[ref[:, width:] for ref in part_refs]).astype(jnp.float32)
    scores = jnp.concatenate([scores, jnp.zeros((lanes - rows, lanes), jnp.float32)], axis=0).T
    expert = lax.broadcasted_iota(jnp.int32, (lanes, rows), 0)
    named = [
        jnp.sum(
            jnp.where(ids_ref[k : k + 1] == expert, scores[:, :rows], 0.0), axis=0, keepdims=True
        )
        for k in range(ids_ref.shape[0])
    ]
    gate_out[...] = jnp.concatenate(named, axis=0).astype(jnp.bfloat16)


def finished(parts, ids, width):
    top, rows = ids.shape
    packed = parts[0].shape[1]
    return pl.pallas_call(
        finish_kernel,
        grid=(1,),
        in_specs=[pl.BlockSpec((rows, packed), lambda i: (0, 0))] * len(parts)
        + [pl.BlockSpec((top, rows), lambda i: (0, 0))],
        out_specs=[
            pl.BlockSpec((rows, width), lambda i: (0, 0)),
            pl.BlockSpec((top, rows), lambda i: (0, 0)),
        ],
        out_shape=[
            jax.ShapeDtypeStruct((rows, width), jnp.bfloat16),
            jax.ShapeDtypeStruct((top, rows), jnp.bfloat16),
        ],
        **kernel_params(0, 0, 0, 8),
    )(*parts, ids)


def dense_body(tokens, expert_ids, gate_weights, cotangent, w_gate, w_up, w_down):
    model_width = tokens.shape[1]
    experts = lax.axis_size("expert")
    groups = lax.axis_size("dp")
    share = w_gate.shape[1] // groups
    place = jnp.stack([lax.axis_index("expert"), lax.axis_index("dp")]).astype(jnp.int32)
    group, core, near, low, high = 1, 2, 4, 8, 16
    lanes = -(-experts // 128) * 128
    named = expert_ids.T[:, :, None] == jnp.arange(lanes, dtype=jnp.int32)[None, None, :]
    gate_table = jnp.sum(
        jnp.where(named, gate_weights.T.astype(jnp.float32)[:, :, None], 0.0), axis=0
    ).astype(jnp.bfloat16)

    def column_of(value):
        return [swap(value, high), swap(value, low), swap(value, low | high)]

    weights = (w_gate, w_up, w_down)
    packed = jnp.concatenate([cotangent, gate_table], axis=1)
    x_high, x_low, x_both = column_of(tokens)
    packed, x_low = tied(packed, x_low)
    cot_mine_away, near_mine_away = swap(packed, group), swap(packed, group | near)
    packed, cot_mine_away, near_mine_away, x_high, x_low, x_both = tied(
        packed, cot_mine_away, near_mine_away, x_high, x_low, x_both
    )
    x_column = jnp.concatenate([tokens, x_high, x_low, x_both], axis=0)
    x_near = swap(x_column, near)
    x_column_away = swap(x_column, group)
    *cot_far, x_near, x_column_away = tied(*column_of(packed), x_near, x_column_away)
    x_near_away = swap(x_near, group)
    cot_column = jnp.concatenate([packed, *cot_far], axis=0)
    cot_high_away = swap(cot_mine_away, high)
    cot_near = swap(cot_column, near)
    *kept_weights, x_rows, slope, swish, hidden = forward(
        [x_column, swap(x_column, core), x_near, swap(x_near, core)], weights
    )
    saved = (slope, swish, hidden)
    own_part, other_part, column_cot, column_lefts, token = backward(
        place, [cot_column, swap(cot_column, core)], saved, 0, kept_weights, place
    )
    column_own, column_given = own_part, swap(other_part, core)
    x_column_other = swap(x_column_away, core)
    cot_near, token, x_near_away, x_column_other, cot_high_away = tied(
        cot_near, token, x_near_away, x_column_other, cot_high_away
    )
    cot_first_away = jnp.concatenate([cot_mine_away, cot_high_away], axis=0)
    cot_second_away, cot_first_other = swap(cot_first_away, low), swap(cot_first_away, core)
    x_near_other = swap(x_near_away, core)
    near_mine_other = swap(near_mine_away, core)
    near_far_away = swap(cot_near[packed.shape[0] :], group)
    half = x_rows.shape[0] // 2
    other_part, other_cot, other_lefts, _ = backward(
        place, [swap(cot_near, core)], saved, half + half // 2, kept_weights, token
    )
    own_part, own_cot, own_lefts, _ = backward(
        place, [cot_near], saved, half, kept_weights, token
    )
    other_part, x_near_other, column_given, cot_first_other, near_mine_other = tied(
        other_part, x_near_other, column_given, cot_first_other, near_mine_other
    )
    near_sum = added(own_part, swap(other_part, core))
    partial = added(column_own, column_given, swap(near_sum, near))
    block = packed.shape[0]
    x_away = [x_column_away, x_near_away, x_column_other, x_near_other]
    *own, slope, swish, hidden, token = own_gradients(
        place,
        [column_lefts, own_lefts, other_lefts],
        x_rows,
        [column_cot, own_cot, other_cot],
        x_away,
        weights[:2],
        share,
    )
    cot_second_away, near_far_away, partial, token = tied(
        cot_second_away, near_far_away, partial, token
    )
    cot_rest_away = jnp.concatenate([cot_second_away, near_far_away], axis=0)
    cot_away = [cot_first_away, near_mine_away, cot_rest_away]
    cot_away += [cot_first_other, near_mine_other, swap(cot_rest_away, core)]
    saved = (slope, swish, hidden)
    grads = list(whole_gradients(place, cot_away, w_down, saved, x_away, own, token))
    parts = [
        partial,
        swap(partial[block : 2 * block], high),
        swap(partial[2 * block : 3 * block], low),
        swap(partial[3 * block :], low | high),
    ]
    *parts, grads[0] = tied(*parts, grads[0])
    token_grad, gate_grad = finished(parts, expert_ids.T, model_width)
    return (token_grad, gate_grad.T, *grads)


def body(tokens, expert_ids, *rest):
    tok_rows, top_count = expert_ids.shape
    sizes = (lax.axis_size("expert"), lax.axis_size("dp"))
    if sizes != (16, 2) or 2 * tok_rows * top_count // sizes[0] < tok_rows:
        return routed_body(tokens, expert_ids, *rest)
    return dense_body(tokens, expert_ids, *rest)


def solution(mesh):
    return jax.shard_map(
        body,
        mesh=mesh,
        in_specs=(
            P(("expert", "dp"), None),
            P(("expert", "dp"), None),
            P(("expert", "dp"), None),
            P(("expert", "dp"), None),
            P("expert", None, None),
            P("expert", None, None),
            P("expert", None, None),
        ),
        out_specs=(
            P(("expert", "dp"), None),
            P(("expert", "dp"), None),
            P("expert", "dp", None),
            P("expert", "dp", None),
            P("expert", "dp", None),
        ),
        check_vma=False,
    )
```
